32 devices in a mesh: blk: 8 (over z, y), vec: 4 (over x, core).
Axes of the slice: x: 2, y: 2, z: 4, core: 2. Of those that a mesh axis runs over, the one named last changes fastest.
Arguments:
- cholesky_factors: bfloat16 [384, 128, 1024], P(('blk', 'vec')), may hold values from -0.1875 to 0.1875
- walker_green: bfloat16 [8, 128, 1024], P('blk'), may hold values from -8 to 8
Outputs:
- exchange_grad: float32 [8, 128, 1024], P('blk', None, 'vec')
- exchange_energy: float32 [8], P('blk')
The draws below stay inside these ranges and needn't reach their ends.
All inputs are finite; a program needn't handle non-finite values.
Results may differ from the reference program's by a relative error of at most 0.0029.
Values may be sent and summed in bfloat16 or wider, within the bound.
A program may use at most 64 MiB of HBM per device.

```python
import math
import jax
import jax.numpy as jnp
from jax import lax

NEL = 128
NORB = 1024
VEC_DEV = 12
NCHOL = 384
WALKERS = 8


def draw_walker_green(key, part):
    base_key, scale_key = jax.random.split(jax.random.fold_in(key, 11))
    entries = jnp.clip(jax.random.normal(base_key, (WALKERS, NEL, NORB), jnp.float32), -4.0, 4.0)
    spread = jnp.exp(jax.random.uniform(scale_key, (WALKERS,), jnp.float32, math.log(0.5), math.log(2.0)))
    return (entries * spread[:, None, None]).astype(jnp.bfloat16)


def shard_levels(key, dims, cuts, least, top_value):
    gain, own = 1.0, jax.random.fold_in(key, 6)
    for position, blocks in cuts:
        heights = jnp.exp(jax.random.uniform(jax.random.fold_in(own, position), (blocks,), jnp.float32, least / len(cuts), top_value / len(cuts)))
        gain = gain * jnp.repeat(heights, dims[position] // blocks).reshape([-1 if axis == position else 1 for axis in range(len(dims))])
    return gain


def normal_values(stream_key, dims, scale, most, cuts=(), dtype=jnp.bfloat16):
    gain = shard_levels(stream_key, dims, cuts, -0.22, 0.18) if cuts else 1.0
    result = jax.random.normal(stream_key, dims, jnp.float32) * scale * gain
    return jnp.minimum(jnp.maximum(result, -most), most).astype(dtype)


def setup_inputs(seed: int = 0) -> dict:
    keys = jax.random.split(jax.random.key(seed), 3)
    cholesky_factors = normal_values(keys[0], (NCHOL, NEL, NORB), NORB ** -0.5, 0.1875, ((0, 32),))
    walker_green = draw_walker_green(jax.random.fold_in(keys[2], 71), 0)
    return {"cholesky_factors": cholesky_factors, "walker_green": walker_green}


def reference(cholesky_factors, walker_green):
    green_f = walker_green.astype(jnp.float32)
    blocks = cholesky_factors.reshape(NCHOL // VEC_DEV, VEC_DEV, NEL, NORB)

    def absorb(running, vector_block):
        vectors_float = vector_block.astype(jnp.float32)
        shared_portion = jnp.einsum('gap,wbp->wgab', vectors_float, green_f)
        rounded_lowprec = lax.optimization_barrier(shared_portion.astype(jnp.bfloat16)).astype(jnp.float32)
        summand_terms = jnp.einsum('vhlr,hrm->vlm', rounded_lowprec, vectors_float)
        return (running + summand_terms, None)
    kernel_sum, unused = lax.scan(absorb, jnp.zeros((WALKERS, NEL, NORB), jnp.float32), blocks)
    energy = -0.5 / (NEL * NCHOL) * lax.optimization_barrier(jnp.sum(kernel_sum * green_f, axis=(1, 2)))
    gradient = kernel_sum / math.sqrt(NCHOL)
    return (gradient, energy)
```

```python
import functools
import math

import jax
import jax.numpy as jnp
from jax import lax
from jax.experimental import pallas as pl
from jax.experimental.pallas import tpu as pltpu
from jax.sharding import PartitionSpec as P

MESH = pl.DeviceIdType.MESH


def flip(value, step, size):
    total, bit = 0, 1
    while bit < size:
        total = total + ((value // bit + step // bit) % 2) * bit
        bit *= 2
    return total


def kernel(
    groups, vec_count, energy_scale, grad_scale,
    l_hbm, g_hbm,
    grad_ref, energy_ref,
    l_ref, gall, inter, core_out, core_in, x_out, x_in, own, y_out, y_in, kept, z_out, z_in, ebuf,
    l_sem, g_sem,
    gz_s, gz_r, gy_s, gy_r, gc0_s, gc0_r, gc1_s, gc1_r,
    rc_s, rc_r, rx_s, rx_r, ry_s, ry_r, rz_s, rz_r, e_s, e_r,
):
    blk, vec = lax.axis_index("blk"), lax.axis_index("vec")
    z, y = blk // 2, blk % 2
    x, c = vec // 2, vec % 2
    el = g_hbm.shape[1]
    norb = g_hbm.shape[2]
    vectors = l_hbm.shape[0]
    quarter = norb // vec_count
    half = norb // 2

    core_peer = {"blk": blk, "vec": x * 2 + (1 - c)}
    x_peer = {"blk": blk, "vec": (1 - x) * 2 + c}
    diagonal = {"blk": blk, "vec": (1 - x) * 2 + (1 - c)}
    y_peer = {"blk": z * 2 + (1 - y), "vec": vec}

    def z_peer(k):
        return {"blk": flip(z, k, groups) * 2 + y, "vec": vec}

    mine = pl.ds(pl.multiple_of(c * half, half), half)
    rows_me = pl.ds(pl.multiple_of(y * el, el), el)
    rows_other = pl.ds(pl.multiple_of((1 - y) * el, el), el)

    def remote(src, dst, s, r, peer):
        return pltpu.make_async_remote_copy(
            src_ref=src, dst_ref=dst, send_sem=s, recv_sem=r, device_id=peer, device_id_type=MESH
        )

    def gz(k):
        return remote(g_hbm.at[0, :, mine], gall.at[k, y, :, mine], gz_s.at[k], gz_r.at[k], z_peer(k))

    def gy_first():
        return remote(g_hbm.at[0, :, mine], gall.at[0, y, :, mine], gy_s.at[0], gy_r.at[0], y_peer)

    def gy(k):
        return remote(
            gall.at[k, y, :, mine], gall.at[k, y, :, mine], gy_s.at[k], gy_r.at[k], y_peer
        )

    def gc0(k):
        return remote(
            gall.at[k, y, :, mine], gall.at[k, y, :, mine], gc0_s.at[k], gc0_r.at[k], core_peer
        )

    def gc1(k):
        return remote(
            gall.at[k, 1 - y, :, mine], gall.at[k, 1 - y, :, mine], gc1_s.at[k], gc1_r.at[k], core_peer
        )

    def rc(k, part):
        return remote(
            core_out.at[k, part], core_in.at[k, part], rc_s.at[k, part], rc_r.at[k, part], core_peer
        )

    def rx(k):
        return remote(x_out.at[k], x_in.at[k], rx_s.at[k], rx_r.at[k], x_peer)

    def ry(k):
        return remote(y_out.at[k], y_in.at[k], ry_s.at[k], ry_r.at[k], y_peer)

    def rz(k):
        return remote(z_out.at[k], z_in.at[k], rz_s.at[k], rz_r.at[k], z_peer(k))

    l_copy = pltpu.make_async_copy(l_hbm, l_ref, l_sem)
    g_copy = pltpu.make_async_copy(g_hbm.at[0], gall.at[0, y], g_sem)
    l_copy.start()
    g_copy.start()

    barrier = pltpu.get_barrier_semaphore()
    for peer in (core_peer, x_peer, diagonal, y_peer):
        pl.semaphore_signal(barrier, inc=1, device_id=peer, device_id_type=MESH)
    for k in range(1, groups):
        pl.semaphore_signal(barrier, inc=1, device_id=z_peer(k), device_id_type=MESH)
    pl.semaphore_wait(barrier, 4 + groups - 1)

    gy_first().start()
    for k in range(1, groups):
        gz(k).start()
    g_copy.wait()
    l_copy.wait()
    gy_first().wait_recv()
    gc1(0).start()

    def columns(xq, cq):
        return pl.ds(pl.multiple_of((xq * 2 + cq) * quarter, quarter), quarter)

    def product(cols):
        return jnp.dot(
            inter[...],
            l_ref[:, :, cols].reshape(vectors * el, quarter),
            preferred_element_type=jnp.float32,
        )

    def y_stage(k):
        rx(k).wait_recv()
        y_out[k] = (
            own[k, rows_other, :] + x_in[k, rows_other, :].astype(jnp.float32)
        ).astype(jnp.bfloat16)
        ry(k).start()
        kept[k] = own[k, rows_me, :] + x_in[k, rows_me, :].astype(jnp.float32)

    def z_stage(k):
        ry(k).wait_recv()
        kept[k] = kept[k] + y_in[k].astype(jnp.float32)

        @pl.when(k > 0)
        def _():
            z_out[k] = kept[k].astype(jnp.bfloat16)
            rz(k).start()

    chunk = math.gcd(vectors, 4)

    def step(k, carry):
        @pl.when(k + 1 < groups)
        def _():
            gz(k + 1).wait_recv()
            gy(k + 1).start()
            gc0(k + 1).start()

        gc1(k).wait_recv()

        @pl.when(k > 0)
        def _():
            gc0(k).wait_recv()

        green = gall[k].reshape(2 * el, norb)
        for first in range(0, vectors, chunk):
            block = lax.dot_general(
                l_ref[first : first + chunk].reshape(chunk * el, norb),
                green,
                (((1,), (1,)), ((), ())),
                preferred_element_type=jnp.float32,
            ).astype(jnp.bfloat16)
            for g in range(chunk):
                for w in range(2):
                    inter[w * el : (w + 1) * el, (first + g) * el : (first + g + 1) * el] = block[
                        g * el : (g + 1) * el, w * el : (w + 1) * el
                    ]

        @pl.when(k > 1)
        def _():
            z_stage(k - 2)

        core_out[k, 0] = product(columns(1 - x, 1 - c)).astype(jnp.bfloat16)
        rc(k, 0).start()
        core_out[k, 1] = product(columns(x, 1 - c)).astype(jnp.bfloat16)
        rc(k, 1).start()
        share = product(columns(1 - x, c))
        rc(k, 0).wait_recv()
        x_out[k] = (share + core_in[k, 0].astype(jnp.float32)).astype(jnp.bfloat16)
        rx(k).start()

        @pl.when(k + 1 < groups)
        def _():
            gy(k + 1).wait_recv()
            gc1(k + 1).start()

        share = product(columns(x, c))
        rc(k, 1).wait_recv()
        own[k] = share + core_in[k, 1].astype(jnp.float32)

        @pl.when(k > 0)
        def _():
            y_stage(k - 1)

        return carry

    lax.fori_loop(0, groups, step, 0)
    last = groups - 1
    z_stage(last - 1)
    y_stage(last)
    z_stage(last)

    total = kept[0]
    for k in range(1, groups):
        rz(k).wait_recv()
        total = total + z_in[k].astype(jnp.float32)
    grad_ref[...] = total * grad_scale

    mine_cols = columns(x, c)
    energy = jnp.sum(total * gall[0, y, :, mine_cols].astype(jnp.float32))
    ebuf[vec] = jnp.full(ebuf.shape[1:], energy, jnp.float32)
    sends = []
    for n, peer in enumerate((core_peer, x_peer, diagonal)):
        copy = remote(ebuf.at[vec], ebuf.at[vec], e_s.at[n], e_r.at[n], peer)
        copy.start()
        sends.append(copy)
    for copy in sends:
        copy.wait_recv()
    energies = ebuf[0]
    for n in range(1, vec_count):
        energies = energies + ebuf[n]
    energy_ref[0] = jnp.max(energies) * energy_scale

    for copy in sends:
        copy.wait_send()

    gy_first().wait_send()
    gc1(0).wait_send()
    for k in range(groups):
        rc(k, 0).wait_send()
        rc(k, 1).wait_send()
        rx(k).wait_send()
        ry(k).wait_send()
        if k > 0:
            gz(k).wait_send()
            gy(k).wait_send()
            gc0(k).wait_send()
            gc1(k).wait_send()
            rz(k).wait_send()


def shards(cholesky_factors, walker_green):
    blk_count = lax.axis_size("blk")
    vec_count = lax.axis_size("vec")
    vectors, el, norb = cholesky_factors.shape
    vector_total = vectors * blk_count * vec_count
    groups = blk_count // 2
    assert vec_count == 4 and groups > 1 and groups & (groups - 1) == 0
    quarter = norb // vec_count
    bf, f32 = jnp.bfloat16, jnp.float32
    dma = pltpu.SemaphoreType.DMA
    flops = 4 * blk_count * vectors * el * el * norb
    gradient, energy = pl.pallas_call(
        functools.partial(
            kernel, groups, vec_count, -0.5 / (el * vector_total), 1.0 / math.sqrt(vector_total)
        ),
        out_shape=(
            jax.ShapeDtypeStruct((el, quarter), f32),
            jax.ShapeDtypeStruct((1,), f32),
        ),
        in_specs=[pl.BlockSpec(memory_space=pl.ANY)] * 2,
        out_specs=(
            pl.BlockSpec(memory_space=pltpu.VMEM),
            pl.BlockSpec(memory_space=pltpu.SMEM),
        ),
        scratch_shapes=[
            pltpu.VMEM((vectors, el, norb), bf),
            pltpu.VMEM((groups, 2, el, norb), bf),
            pltpu.VMEM((2 * el, vectors * el), bf),
            pltpu.VMEM((groups, 2, 2 * el, quarter), bf),
            pltpu.VMEM((groups, 2, 2 * el, quarter), bf),
            pltpu.VMEM((groups, 2 * el, quarter), bf),
            pltpu.VMEM((groups, 2 * el, quarter), bf),
            pltpu.VMEM((groups, 2 * el, quarter), f32),
            pltpu.VMEM((groups, el, quarter), bf),
            pltpu.VMEM((groups, el, quarter), bf),
            pltpu.VMEM((groups, el, quarter), f32),
            pltpu.VMEM((groups, el, quarter), bf),
            pltpu.VMEM((groups, el, quarter), bf),
            pltpu.VMEM((vec_count, 8, 128), f32),
            dma, dma,
        ]
        + [dma((groups,))] * 8
        + [dma((groups, 2))] * 2
        + [dma((groups,))] * 6
        + [dma((3,))] * 2,
        compiler_params=pltpu.CompilerParams(
            collective_id=0, has_side_effects=True, vmem_limit_bytes=56 * 1024 * 1024
        ),
        cost_estimate=pl.CostEstimate(
            flops=flops, bytes_accessed=2 * vectors * el * norb, transcendentals=0
        ),
        name="exchange",
    )(cholesky_factors, walker_green)
    return gradient[None], energy


def solution(mesh):
    return jax.shard_map(
        shards,
        mesh=mesh,
        in_specs=(P(("blk", "vec"), None, None), P("blk", None, None)),
        out_specs=(P("blk", None, "vec"), P("blk")),
        check_vma=False,
    )
```

```python
import functools
import math

import jax
import jax.numpy as jnp
from jax import lax
from jax.experimental import pallas as pl
from jax.experimental.pallas import tpu as pltpu
from jax.sharding import PartitionSpec as P

MESH = pl.DeviceIdType.MESH


def flip(value, step, size):
    total, bit = 0, 1
    while bit < size:
        total = total + ((value // bit + step // bit) % 2) * bit
        bit *= 2
    return total


def kernel(
    groups, vec_count, energy_scale, grad_scale,
    l_hbm, g_hbm,
    grad_ref, energy_ref,
    l_ref, gall, inter, core_out, core_in, x_out, x_in, own, y_out, y_in, kept, z_out, z_in, ebuf, e_in,
    l_sem, g_sem,
    gz_s, gz_r, gx_s, gx_r, gc0_s, gc0_r, gc1_s, gc1_r, ry_s, ry_r, rz_s, rz_r,
    gy_s, gy_r, rc_s, rc_r, rx_s, rx_r, e_s, e_r,
):
    blk, vec = lax.axis_index("blk"), lax.axis_index("vec")
    z, y = blk // 2, blk % 2
    x, c = vec // 2, vec % 2
    el = g_hbm.shape[1]
    norb = g_hbm.shape[2]
    vectors = l_hbm.shape[0]
    quarter = norb // vec_count
    half = norb // 2

    core_peer = {"blk": blk, "vec": x * 2 + (1 - c)}
    x_peer = {"blk": blk, "vec": (1 - x) * 2 + c}
    y_peer = {"blk": z * 2 + (1 - y), "vec": vec}

    def z_peer(k):
        return {"blk": flip(z, k, groups) * 2 + y, "vec": vec}

    def home(k, j):
        return {"blk": flip(z, k, groups) * 2 + y, "vec": flip(vec, j, vec_count)}

    mine = pl.ds(pl.multiple_of(c * half, half), half)
    part_me = pl.ds(pl.multiple_of(c * half + x * quarter, quarter), quarter)
    part_other = pl.ds(pl.multiple_of(c * half + (1 - x) * quarter, quarter), quarter)
    rows_me = pl.ds(pl.multiple_of(y * el, el), el)
    rows_other = pl.ds(pl.multiple_of((1 - y) * el, el), el)

    def remote(src, dst, s, r, peer):
        return pltpu.make_async_remote_copy(
            src_ref=src, dst_ref=dst, send_sem=s, recv_sem=r, device_id=peer, device_id_type=MESH
        )

    def gz(k):
        return remote(
            g_hbm.at[0, :, part_me], gall.at[k, y, :, part_me], gz_s.at[k], gz_r.at[k], z_peer(k)
        )

    def gx(k):
        return remote(
            gall.at[k, y, :, part_me], gall.at[k, y, :, part_me], gx_s.at[k], gx_r.at[k], x_peer
        )

    def gy_first():
        return remote(
            g_hbm.at[0, :, mine], gall.at[0, y, :, mine], gy_s.at[0, 0], gy_r.at[0, 0], y_peer
        )

    def gy(k, n):
        part = (part_me, part_other)[n]
        return remote(
            gall.at[k, y, :, part], gall.at[k, y, :, part], gy_s.at[k, n], gy_r.at[k, n], y_peer
        )

    def gc0(k):
        return remote(
            gall.at[k, y, :, mine], gall.at[k, y, :, mine], gc0_s.at[k], gc0_r.at[k], core_peer
        )

    def gc1(k):
        return remote(
            gall.at[k, 1 - y, :, mine], gall.at[k, 1 - y, :, mine], gc1_s.at[k], gc1_r.at[k], core_peer
        )

    def rc(k, part):
        return remote(
            core_out.at[k, part], core_in.at[k, part], rc_s.at[k, part], rc_r.at[k, part], core_peer
        )

    def rx(k, n):
        rows = (rows_other, rows_me)[n]
        return remote(
            x_out.at[k, rows], x_in.at[k, rows], rx_s.at[k, n], rx_r.at[k, n], x_peer
        )

    def ry(k):
        return remote(y_out.at[k], y_in.at[k], ry_s.at[k], ry_r.at[k], y_peer)

    def rz(k):
        return remote(z_out.at[k], z_in.at[k], rz_s.at[k], rz_r.at[k], z_peer(k))

    def energy_send(k, j):
        return remote(
            ebuf.at[k, vec], e_in.at[k, vec], e_s.at[k, j], e_r.at[k, j], home(k, j)
        )

    l_copy = pltpu.make_async_copy(l_hbm, l_ref, l_sem)
    g_copy = pltpu.make_async_copy(g_hbm.at[0], gall.at[0, y], g_sem)
    l_copy.start()
    g_copy.start()

    barrier = pltpu.get_barrier_semaphore()
    pl.semaphore_signal(barrier, inc=1, device_id=y_peer, device_id_type=MESH)
    for k in range(groups):
        for j in range(vec_count):
            if k + j > 0:
                pl.semaphore_signal(barrier, inc=1, device_id=home(k, j), device_id_type=MESH)
    pl.semaphore_wait(barrier, groups * vec_count)

    gy_first().start()
    for k in range(1, groups):
        gz(k).start()

    def first_service(k):
        gz(k).wait_recv()
        gx(k).start()
        gy(k, 0).start()

    def second_service(k):
        gx(k).wait_recv()
        gy(k, 1).start()
        gc0(k).start()

    def third_service(k):
        gy(k, 0).wait_recv()
        gy(k, 1).wait_recv()
        gc1(k).start()

    first_service(1)
    gy_first().wait_recv()
    gc1(0).start()
    second_service(1)
    if groups > 2:
        first_service(2)
    g_copy.wait()
    l_copy.wait()

    def columns(xq, cq):
        return pl.ds(pl.multiple_of((xq * 2 + cq) * quarter, quarter), quarter)

    def product(cols):
        return jnp.dot(
            inter[...],
            l_ref[:, :, cols].reshape(vectors * el, quarter),
            preferred_element_type=jnp.float32,
        )

    def y_stage(k):
        rx(k, 0).wait_recv()
        y_out[k] = (
            own[k, rows_other, :] + x_in[k, rows_other, :].astype(jnp.float32)
        ).astype(jnp.bfloat16)
        ry(k).start()
        rx(k, 1).wait_recv()
        kept[k] = own[k, rows_me, :] + x_in[k, rows_me, :].astype(jnp.float32)

    def z_stage(k):
        ry(k).wait_recv()
        kept[k] = kept[k] + y_in[k].astype(jnp.float32)

        @pl.when(k > 0)
        def _():
            z_out[k] = kept[k].astype(jnp.bfloat16)
            rz(k).start()

        energy = jnp.sum(kept[k] * gall[k, y, :, columns(x, c)].astype(jnp.float32))
        ebuf[k, vec] = jnp.full(ebuf.shape[2:], energy, jnp.float32)
        for j in range(1, vec_count):
            energy_send(k, j).start()

        @pl.when(k > 0)
        def _():
            energy_send(k, 0).start()

    chunk = math.gcd(vectors, 4)

    def step(k, carry):
        gc1(k).wait_recv()

        @pl.when(k > 0)
        def _():
            gc0(k).wait_recv()

        green = gall[k].reshape(2 * el, norb)
        for first in range(0, vectors, chunk):
            block = lax.dot_general(
                l_ref[first : first + chunk].reshape(chunk * el, norb),
                green,
                (((1,), (1,)), ((), ())),
                preferred_element_type=jnp.float32,
            ).astype(jnp.bfloat16)
            for g in range(chunk):
                for w in range(2):
                    inter[w * el : (w + 1) * el, (first + g) * el : (first + g + 1) * el] = block[
                        g * el : (g + 1) * el, w * el : (w + 1) * el
                    ]

        @pl.when(k + 3 < groups)
        def _():
            first_service(k + 3)

        @pl.when(k > 1)
        def _():
            z_stage(k - 2)

        core_out[k, 0] = product(columns(1 - x, 1 - c)).astype(jnp.bfloat16)
        rc(k, 0).start()
        core_out[k, 1] = product(columns(x, 1 - c)).astype(jnp.bfloat16)
        rc(k, 1).start()
        share = product(columns(1 - x, c))
        rc(k, 0).wait_recv()
        x_out[k] = (share + core_in[k, 0].astype(jnp.float32)).astype(jnp.bfloat16)
        rx(k, 0).start()
        rx(k, 1).start()

        @pl.when(k + 1 < groups)
        def _():
            third_service(k + 1)

        share = product(columns(x, c))
        rc(k, 1).wait_recv()
        own[k] = share + core_in[k, 1].astype(jnp.float32)

        @pl.when(k + 2 < groups)
        def _():
            second_service(k + 2)

        @pl.when(k > 0)
        def _():
            y_stage(k - 1)

        return carry

    lax.fori_loop(0, groups, step, 0)
    last = groups - 1
    y_stage(last)
    z_stage(last - 1)
    z_stage(last)

    total = kept[0]
    for k in range(1, groups):
        rz(k).wait_recv()
        total = total + z_in[k].astype(jnp.float32)
    grad_ref[...] = total * grad_scale

    e_in[0, vec] = ebuf[0, vec]
    for k in range(groups):
        for j in range(vec_count):
            if k + j > 0:
                energy_send(k, j).wait_recv()
    energies = jnp.zeros(e_in.shape[2:], jnp.float32)
    for k in range(groups):
        for n in range(vec_count):
            energies = energies + e_in[k, n]
    energy_ref[0] = jnp.max(energies) * energy_scale

    gy_first().wait_send()
    gc1(0).wait_send()
    for k in range(groups):
        for n in range(2):
            rc(k, n).wait_send()
            rx(k, n).wait_send()
        ry(k).wait_send()
        for j in range(vec_count):
            if k + j > 0:
                energy_send(k, j).wait_send()
        if k > 0:
            gz(k).wait_send()
            gx(k).wait_send()
            gy(k, 0).wait_send()
            gy(k, 1).wait_send()
            gc0(k).wait_send()
            gc1(k).wait_send()
            rz(k).wait_send()


def shards(cholesky_factors, walker_green):
    blk_count = lax.axis_size("blk")
    vec_count = lax.axis_size("vec")
    vectors, el, norb = cholesky_factors.shape
    vector_total = vectors * blk_count * vec_count
    groups = blk_count // 2
    assert vec_count == 4 and groups > 1 and groups & (groups - 1) == 0
    quarter = norb // vec_count
    bf, f32 = jnp.bfloat16, jnp.float32
    dma = pltpu.SemaphoreType.DMA
    flops = 4 * blk_count * vectors * el * el * norb
    gradient, energy = pl.pallas_call(
        functools.partial(
            kernel, groups, vec_count, -0.5 / (el * vector_total), 1.0 / math.sqrt(vector_total)
        ),
        out_shape=(
            jax.ShapeDtypeStruct((el, quarter), f32),
            jax.ShapeDtypeStruct((1,), f32),
        ),
        in_specs=[pl.BlockSpec(memory_space=pl.ANY)] * 2,
        out_specs=(
            pl.BlockSpec(memory_space=pltpu.VMEM),
            pl.BlockSpec(memory_space=pltpu.SMEM),
        ),
        scratch_shapes=[
            pltpu.VMEM((vectors, el, norb), bf),
            pltpu.VMEM((groups, 2, el, norb), bf),
            pltpu.VMEM((2 * el, vectors * el), bf),
            pltpu.VMEM((groups, 2, 2 * el, quarter), bf),
            pltpu.VMEM((groups, 2, 2 * el, quarter), bf),
            pltpu.VMEM((groups, 2 * el, quarter), bf),
            pltpu.VMEM((groups, 2 * el, quarter), bf),
            pltpu.VMEM((groups, 2 * el, quarter), f32),
            pltpu.VMEM((groups, el, quarter), bf),
            pltpu.VMEM((groups, el, quarter), bf),
            pltpu.VMEM((groups, el, quarter), f32),
            pltpu.VMEM((groups, el, quarter), bf),
            pltpu.VMEM((groups, el, quarter), bf),
            pltpu.VMEM((groups, vec_count, 8, 128), f32),
            pltpu.VMEM((groups, vec_count, 8, 128), f32),
            dma, dma,
        ]
        + [dma((groups,))] * 12
        + [dma((groups, 2))] * 6
        + [dma((groups, vec_count))] * 2,
        compiler_params=pltpu.CompilerParams(
            collective_id=0, has_side_effects=True, vmem_limit_bytes=56 * 1024 * 1024
        ),
        cost_estimate=pl.CostEstimate(
            flops=flops, bytes_accessed=2 * vectors * el * norb, transcendentals=0
        ),
        name="exchange",
    )(cholesky_factors, walker_green)
    return gradient[None], energy


def solution(mesh):
    return jax.shard_map(
        shards,
        mesh=mesh,
        in_specs=(P(("blk", "vec"), None, None), P("blk", None, None)),
        out_specs=(P("blk", None, "vec"), P("blk")),
        check_vma=False,
    )
```

```python
import functools
import math

import jax
import jax.numpy as jnp
from jax import lax
from jax.experimental import pallas as pl
from jax.experimental.pallas import tpu as pltpu
from jax.sharding import PartitionSpec as P

MESH = pl.DeviceIdType.MESH


def flip(value, step, size):
    total, bit = 0, 1
    while bit < size:
        total = total + ((value // bit + step // bit) % 2) * bit
        bit *= 2
    return total


def kernel(
    groups, vec_count, energy_scale, grad_scale,
    l_hbm, g_hbm,
    grad_ref, energy_ref,
    l_ref, gall, inter, prod, core_out, core_in, x_out, x_in, own, y_out, y_in, kept, z_out, z_in, ebuf, e_in,
    l_sem, g_sem,
    gz_s, gz_r, gx_s, gx_r, gc0_s, gc0_r, gc1_s, gc1_r, ry_s, ry_r, rz_s, rz_r,
    gy_s, gy_r, rc_s, rc_r, rx_s, rx_r, e_s, e_r,
):
    blk, vec = lax.axis_index("blk"), lax.axis_index("vec")
    z, y = blk // 2, blk % 2
    x, c = vec // 2, vec % 2
    el = g_hbm.shape[1]
    norb = g_hbm.shape[2]
    vectors = l_hbm.shape[0]
    quarter = norb // vec_count
    half = norb // 2

    core_peer = {"blk": blk, "vec": x * 2 + (1 - c)}
    x_peer = {"blk": blk, "vec": (1 - x) * 2 + c}
    y_peer = {"blk": z * 2 + (1 - y), "vec": vec}

    def z_peer(k):
        return {"blk": flip(z, k, groups) * 2 + y, "vec": vec}

    def home(k, j):
        return {"blk": flip(z, k, groups) * 2 + y, "vec": flip(vec, j, vec_count)}

    mine = pl.ds(pl.multiple_of(c * half, half), half)
    part_me = pl.ds(pl.multiple_of(c * half + x * quarter, quarter), quarter)
    part_other = pl.ds(pl.multiple_of(c * half + (1 - x) * quarter, quarter), quarter)
    rows_me = pl.ds(pl.multiple_of(y * el, el), el)
    rows_other = pl.ds(pl.multiple_of((1 - y) * el, el), el)

    def remote(src, dst, s, r, peer):
        return pltpu.make_async_remote_copy(
            src_ref=src, dst_ref=dst, send_sem=s, recv_sem=r, device_id=peer, device_id_type=MESH
        )

    def gz(k):
        return remote(
            g_hbm.at[0, :, part_me], gall.at[k, y, :, part_me], gz_s.at[k], gz_r.at[k], z_peer(k)
        )

    def gx(k):
        return remote(
            gall.at[k, y, :, part_me], gall.at[k, y, :, part_me], gx_s.at[k], gx_r.at[k], x_peer
        )

    def gy_first():
        return remote(
            g_hbm.at[0, :, mine], gall.at[0, y, :, mine], gy_s.at[0, 0], gy_r.at[0, 0], y_peer
        )

    def gy(k, n):
        part = (part_me, part_other)[n]
        return remote(
            gall.at[k, y, :, part], gall.at[k, y, :, part], gy_s.at[k, n], gy_r.at[k, n], y_peer
        )

    def gc0(k):
        return remote(
            gall.at[k, y, :, mine], gall.at[k, y, :, mine], gc0_s.at[k], gc0_r.at[k], core_peer
        )

    def gc1(k):
        return remote(
            gall.at[k, 1 - y, :, mine], gall.at[k, 1 - y, :, mine], gc1_s.at[k], gc1_r.at[k], core_peer
        )

    def rc(k, part):
        return remote(
            core_out.at[k, part], core_in.at[k, part], rc_s.at[k, part], rc_r.at[k, part], core_peer
        )

    def rx(k, n):
        rows = (rows_other, rows_me)[n]
        return remote(
            x_out.at[k, rows], x_in.at[k, rows], rx_s.at[k, n], rx_r.at[k, n], x_peer
        )

    def ry(k):
        return remote(y_out.at[k], y_in.at[k], ry_s.at[k], ry_r.at[k], y_peer)

    def rz(k):
        return remote(z_out.at[k], z_in.at[k], rz_s.at[k], rz_r.at[k], z_peer(k))

    def energy_send(k, j):
        return remote(
            ebuf.at[k, vec], e_in.at[k, vec], e_s.at[k, j], e_r.at[k, j], home(k, j)
        )

    l_copy = pltpu.make_async_copy(l_hbm, l_ref, l_sem)
    g_copy = pltpu.make_async_copy(g_hbm.at[0], gall.at[0, y], g_sem)
    l_copy.start()
    g_copy.start()

    barrier = pltpu.get_barrier_semaphore()
    pl.semaphore_signal(barrier, inc=1, device_id=y_peer, device_id_type=MESH)
    for k in range(groups):
        for j in range(vec_count):
            if k + j > 0:
                pl.semaphore_signal(barrier, inc=1, device_id=home(k, j), device_id_type=MESH)
    pl.semaphore_wait(barrier, groups * vec_count)

    gy_first().start()
    for k in range(1, groups):
        gz(k).start()

    def first_service(k):
        gz(k).wait_recv()
        gx(k).start()
        gy(k, 0).start()

    def second_service(k):
        gx(k).wait_recv()
        gy(k, 1).start()
        gc0(k).start()

    def third_service(k):
        gy(k, 0).wait_recv()
        gy(k, 1).wait_recv()
        gc1(k).start()

    first_service(1)
    gy_first().wait_recv()
    gc1(0).start()
    second_service(1)
    if groups > 2:
        first_service(2)
    third_service(1)
    g_copy.wait()
    l_copy.wait()

    def columns(xq, cq):
        return pl.ds(pl.multiple_of((xq * 2 + cq) * quarter, quarter), quarter)

    def product(h, xq):
        cols = pl.ds(pl.multiple_of(xq * half, half), half)
        prod[...] = jnp.dot(
            inter[h * 2 * el : (h + 1) * 2 * el, :],
            l_ref[:, :, cols].reshape(vectors * el, half),
            preferred_element_type=jnp.float32,
        )

    def prod_part(cq):
        return prod[:, pl.ds(pl.multiple_of(cq * quarter, quarter), quarter)]

    def y_stage(k):
        rx(k, 0).wait_recv()
        y_out[k] = (
            own[k, rows_other, :] + x_in[k, rows_other, :].astype(jnp.float32)
        ).astype(jnp.bfloat16)
        ry(k).start()
        rx(k, 1).wait_recv()
        kept[k] = own[k, rows_me, :] + x_in[k, rows_me, :].astype(jnp.float32)

    def z_stage(k):
        ry(k).wait_recv()
        kept[k] = kept[k] + y_in[k].astype(jnp.float32)

        @pl.when(k > 0)
        def _():
            z_out[k] = kept[k].astype(jnp.bfloat16)
            rz(k).start()

        energy = jnp.sum(kept[k] * gall[k, y, :, columns(x, c)].astype(jnp.float32))
        ebuf[k, vec] = jnp.full(ebuf.shape[2:], energy, jnp.float32)
        for j in range(1, vec_count):
            energy_send(k, j).start()

        @pl.when(k > 0)
        def _():
            energy_send(k, 0).start()

    chunk = math.gcd(vectors, 4)

    def step(pair, carry):
        base = 2 * pair
        more = base + 2 < groups
        for h in range(2):
            gc1(base + h).wait_recv()
        gc0(base + 1).wait_recv()

        @pl.when(pair > 0)
        def _():
            gc0(base).wait_recv()

        @pl.when(more)
        def _():
            second_service(base + 2)
            first_service(base + 3)

        for first in range(0, vectors, chunk):
            block = lax.dot_general(
                l_ref[first : first + chunk].reshape(chunk * el, norb),
                gall[pl.ds(base, 2)].reshape(4 * el, norb),
                (((1,), (1,)), ((), ())),
                preferred_element_type=jnp.float32,
            ).astype(jnp.bfloat16)
            for g in range(chunk):
                for w in range(4):
                    inter[w * el : (w + 1) * el, (first + g) * el : (first + g + 1) * el] = block[
                        g * el : (g + 1) * el, w * el : (w + 1) * el
                    ]

        for h in range(2):
            k = base + h

            @pl.when(k > 1)
            def _():
                z_stage(k - 2)

            product(h, 1 - x)
            core_out[k, 0] = prod_part(1 - c).astype(jnp.bfloat16)
            rc(k, 0).start()
            own[k] = prod_part(c)
            product(h, x)
            core_out[k, 1] = prod_part(1 - c).astype(jnp.bfloat16)
            rc(k, 1).start()
            rc(k, 0).wait_recv()
            x_out[k] = (own[k] + core_in[k, 0].astype(jnp.float32)).astype(jnp.bfloat16)
            rx(k, 0).start()
            rx(k, 1).start()

            @pl.when(more)
            def _():
                if h == 0:
                    second_service(base + 3)
                    third_service(base + 2)
                else:
                    third_service(base + 3)

            if h == 1:

                @pl.when(base + 4 < groups)
                def _():
                    first_service(base + 4)

            rc(k, 1).wait_recv()
            own[k] = prod_part(c) + core_in[k, 1].astype(jnp.float32)

            @pl.when(k > 0)
            def _():
                y_stage(k - 1)

        return carry

    lax.fori_loop(0, groups // 2, step, 0)
    last = groups - 1
    y_stage(last)
    z_stage(last - 1)
    z_stage(last)

    total = kept[0]
    for k in range(1, groups):
        rz(k).wait_recv()
        total = total + z_in[k].astype(jnp.float32)
    grad_ref[...] = total * grad_scale

    e_in[0, vec] = ebuf[0, vec]
    for k in range(groups):
        for j in range(vec_count):
            if k + j > 0:
                energy_send(k, j).wait_recv()
    energies = jnp.zeros(e_in.shape[2:], jnp.float32)
    for k in range(groups):
        for n in range(vec_count):
            energies = energies + e_in[k, n]
    energy_ref[0] = jnp.max(energies) * energy_scale

    gy_first().wait_send()
    gc1(0).wait_send()
    for k in range(groups):
        for n in range(2):
            rc(k, n).wait_send()
            rx(k, n).wait_send()
        ry(k).wait_send()
        for j in range(vec_count):
            if k + j > 0:
                energy_send(k, j).wait_send()
        if k > 0:
            gz(k).wait_send()
            gx(k).wait_send()
            gy(k, 0).wait_send()
            gy(k, 1).wait_send()
            gc0(k).wait_send()
            gc1(k).wait_send()
            rz(k).wait_send()


def shards(cholesky_factors, walker_green):
    blk_count = lax.axis_size("blk")
    vec_count = lax.axis_size("vec")
    vectors, el, norb = cholesky_factors.shape
    vector_total = vectors * blk_count * vec_count
    groups = blk_count // 2
    assert vec_count == 4 and groups > 1 and groups & (groups - 1) == 0
    quarter = norb // vec_count
    bf, f32 = jnp.bfloat16, jnp.float32
    dma = pltpu.SemaphoreType.DMA
    flops = 4 * blk_count * vectors * el * el * norb
    gradient, energy = pl.pallas_call(
        functools.partial(
            kernel, groups, vec_count, -0.5 / (el * vector_total), 1.0 / math.sqrt(vector_total)
        ),
        out_shape=(
            jax.ShapeDtypeStruct((el, quarter), f32),
            jax.ShapeDtypeStruct((1,), f32),
        ),
        in_specs=[pl.BlockSpec(memory_space=pl.ANY)] * 2,
        out_specs=(
            pl.BlockSpec(memory_space=pltpu.VMEM),
            pl.BlockSpec(memory_space=pltpu.SMEM),
        ),
        scratch_shapes=[
            pltpu.VMEM((vectors, el, norb), bf),
            pltpu.VMEM((groups, 2, el, norb), bf),
            pltpu.VMEM((4 * el, vectors * el), bf),
            pltpu.VMEM((2 * el, norb // 2), f32),
            pltpu.VMEM((groups, 2, 2 * el, quarter), bf),
            pltpu.VMEM((groups, 2, 2 * el, quarter), bf),
            pltpu.VMEM((groups, 2 * el, quarter), bf),
            pltpu.VMEM((groups, 2 * el, quarter), bf),
            pltpu.VMEM((groups, 2 * el, quarter), f32),
            pltpu.VMEM((groups, el, quarter), bf),
            pltpu.VMEM((groups, el, quarter), bf),
            pltpu.VMEM((groups, el, quarter), f32),
            pltpu.VMEM((groups, el, quarter), bf),
            pltpu.VMEM((groups, el, quarter), bf),
            pltpu.VMEM((groups, vec_count, 8, 128), f32),
            pltpu.VMEM((groups, vec_count, 8, 128), f32),
            dma, dma,
        ]
        + [dma((groups,))] * 12
        + [dma((groups, 2))] * 6
        + [dma((groups, vec_count))] * 2,
        compiler_params=pltpu.CompilerParams(
            collective_id=0, has_side_effects=True, vmem_limit_bytes=56 * 1024 * 1024
        ),
        cost_estimate=pl.CostEstimate(
            flops=flops, bytes_accessed=2 * vectors * el * norb, transcendentals=0
        ),
        name="exchange",
    )(cholesky_factors, walker_green)
    return gradient[None], energy


def solution(mesh):
    return jax.shard_map(
        shards,
        mesh=mesh,
        in_specs=(P(("blk", "vec"), None, None), P("blk", None, None)),
        out_specs=(P("blk", None, "vec"), P("blk")),
        check_vma=False,
    )
```

```python
import functools
import math

import jax
import jax.numpy as jnp
from jax import lax
from jax.experimental import pallas as pl
from jax.experimental.pallas import tpu as pltpu
from jax.sharding import PartitionSpec as P

MESH = pl.DeviceIdType.MESH


def flip(value, step, size):
    total, bit = 0, 1
    while bit < size:
        total = total + ((value // bit + step // bit) % 2) * bit
        bit *= 2
    return total


def places(groups, vec_count):
    blk, vec = lax.axis_index("blk"), lax.axis_index("vec")
    z, y = blk // 2, blk % 2
    x, c = vec // 2, vec % 2
    core_peer = {"blk": blk, "vec": x * 2 + (1 - c)}
    x_peer = {"blk": blk, "vec": (1 - x) * 2 + c}
    y_peer = {"blk": z * 2 + (1 - y), "vec": vec}

    def home(k, j):
        return {"blk": flip(z, k, groups) * 2 + y, "vec": flip(vec, j, vec_count)}

    return vec, y, x, c, core_peer, x_peer, y_peer, home


def remote(src, dst, s, r, peer):
    return pltpu.make_async_remote_copy(
        src_ref=src, dst_ref=dst, send_sem=s, recv_sem=r, device_id=peer, device_id_type=MESH
    )


def meet(peers):
    barrier = pltpu.get_barrier_semaphore()
    for peer in peers:
        pl.semaphore_signal(barrier, inc=1, device_id=peer, device_id_type=MESH)
    pl.semaphore_wait(barrier, len(peers))


def gather_kernel(
    groups, vec_count, g_hbm, gall, g_sem,
    gz_s, gz_r, gx_s, gx_r, gc0_s, gc0_r, gc1_s, gc1_r, gy_s, gy_r,
):
    vec, y, x, c, core_peer, x_peer, y_peer, home = places(groups, vec_count)
    norb = g_hbm.shape[2]
    half, quarter = norb // 2, norb // vec_count
    mine = pl.ds(pl.multiple_of(c * half, half), half)
    part_me = pl.ds(pl.multiple_of(c * half + x * quarter, quarter), quarter)
    part_other = pl.ds(pl.multiple_of(c * half + (1 - x) * quarter, quarter), quarter)

    def gz(k):
        return remote(
            g_hbm.at[0, :, part_me], gall.at[k, y, :, part_me], gz_s.at[k], gz_r.at[k], home(k, 0)
        )

    def gx(k):
        view = gall.at[k, y, :, part_me]
        return remote(view, view, gx_s.at[k], gx_r.at[k], x_peer)

    def gy_first():
        return remote(
            g_hbm.at[0, :, mine], gall.at[0, y, :, mine], gy_s.at[0, 0], gy_r.at[0, 0], y_peer
        )

    def gy(k, n):
        view = gall.at[k, y, :, (part_me, part_other)[n]]
        return remote(view, view, gy_s.at[k, n], gy_r.at[k, n], y_peer)

    def gc0(k):
        view = gall.at[k, y, :, mine]
        return remote(view, view, gc0_s.at[k], gc0_r.at[k], core_peer)

    def gc1(k):
        view = gall.at[k, 1 - y, :, mine]
        return remote(view, view, gc1_s.at[k], gc1_r.at[k], core_peer)

    g_copy = pltpu.make_async_copy(g_hbm.at[0], gall.at[0, y], g_sem)
    g_copy.start()
    meet([core_peer, x_peer, y_peer] + [home(k, 0) for k in range(1, groups)])
    gy_first().start()
    for k in range(1, groups):
        gz(k).start()
    for k in range(1, groups):
        gz(k).wait_recv()
        gx(k).start()
        gy(k, 0).start()
    gy_first().wait_recv()
    gc1(0).start()
    for k in range(1, groups):
        gx(k).wait_recv()
        gy(k, 1).start()
        gc0(k).start()
    for k in range(1, groups):
        gy(k, 0).wait_recv()
        gy(k, 1).wait_recv()
        gc1(k).start()
    g_copy.wait()
    gy_first().wait_send()
    gc1(0).wait()
    for k in range(1, groups):
        gc0(k).wait()
        gc1(k).wait()
        gz(k).wait_send()
        gx(k).wait_send()
        gy(k, 0).wait_send()
        gy(k, 1).wait_send()


def reduce_kernel(
    groups, vec_count, energy_scale, grad_scale,
    p_hbm, gall,
    grad_ref, energy_ref,
    part, green, core_out, core_in, x_out, x_in, y_out, y_in, kept, z_out, z_in, ebuf, e_in,
    p_sem, g_sem, ry_s, ry_r, rz_s, rz_r, rc_s, rc_r, rx_s, rx_r, e_s, e_r,
):
    vec, y, x, c, core_peer, x_peer, y_peer, home = places(groups, vec_count)
    el, norb = gall.shape[2], gall.shape[3]
    quarter = norb // vec_count

    def columns(xq, cq):
        return pl.ds(pl.multiple_of((xq * 2 + cq) * quarter, quarter), quarter)

    def rc(k, n):
        return remote(
            core_out.at[k, n], core_in.at[k, n], rc_s.at[k, n], rc_r.at[k, n], core_peer
        )

    def rx(k, n):
        return remote(x_out.at[k, n], x_in.at[k, n], rx_s.at[k, n], rx_r.at[k, n], x_peer)

    def ry(k):
        return remote(y_out.at[k], y_in.at[k], ry_s.at[k], ry_r.at[k], y_peer)

    def rz(k):
        return remote(z_out.at[k], z_in.at[k], rz_s.at[k], rz_r.at[k], home(k, 0))

    def energy_send(k, j):
        return remote(
            ebuf.at[k, vec], e_in.at[k, vec], e_s.at[k, j], e_r.at[k, j], home(k, j)
        )

    def p_copy(k):
        return pltpu.make_async_copy(p_hbm.at[k], part.at[k], p_sem.at[k])

    g_copy = pltpu.make_async_copy(gall.at[:, y, :, columns(x, c)], green, g_sem)
    order = list(range(1, groups)) + [0]
    for k in order:
        p_copy(k).start()
    g_copy.start()
    meet(
        [y_peer]
        + [home(k, j) for k in range(groups) for j in range(vec_count) if k + j > 0]
    )
    f32, bf = jnp.float32, jnp.bfloat16
    for k in order:
        p_copy(k).wait()
        for n, xq in enumerate((1 - x, x)):
            core_out[k, n] = part[k, :, :, columns(xq, 1 - c)].astype(bf)
            rc(k, n).start()
    for k in order:
        rc(k, 0).wait_recv()
        for n, yq in enumerate((1 - y, y)):
            x_out[k, n] = (
                part[k, yq, :, columns(1 - x, c)] + core_in[k, 0, yq].astype(f32)
            ).astype(bf)
            rx(k, n).start()
    g_copy.wait()
    for k in order:
        rc(k, 1).wait_recv()
        rx(k, 0).wait_recv()
        y_out[k] = (
            part[k, 1 - y, :, columns(x, c)]
            + core_in[k, 1, 1 - y].astype(f32)
            + x_in[k, 0].astype(f32)
        ).astype(bf)
        ry(k).start()
    for k in order:
        rx(k, 1).wait_recv()
        ry(k).wait_recv()
        kept[k] = (
            part[k, y, :, columns(x, c)]
            + core_in[k, 1, y].astype(f32)
            + x_in[k, 1].astype(f32)
            + y_in[k].astype(f32)
        )
        if k > 0:
            z_out[k] = kept[k].astype(bf)
            rz(k).start()
        energy = jnp.sum(kept[k] * green[k].astype(f32))
        ebuf[k, vec] = jnp.full(ebuf.shape[2:], energy, f32)
        for j in range(vec_count):
            if k + j > 0:
                energy_send(k, j).start()

    total = kept[0]
    for k in range(1, groups):
        rz(k).wait_recv()
        total = total + z_in[k].astype(f32)
    grad_ref[...] = total * grad_scale

    e_in[0, vec] = ebuf[0, vec]
    for k in range(groups):
        for j in range(vec_count):
            if k + j > 0:
                energy_send(k, j).wait_recv()
    energies = jnp.zeros(e_in.shape[2:], f32)
    for k in range(groups):
        for n in range(vec_count):
            energies = energies + e_in[k, n]
    energy_ref[0] = jnp.max(energies) * energy_scale
    for k in range(groups):
        for n in range(2):
            rc(k, n).wait_send()
            rx(k, n).wait_send()
        ry(k).wait_send()
        for j in range(vec_count):
            if k + j > 0:
                energy_send(k, j).wait_send()
        if k > 0:
            rz(k).wait_send()


def shards(cholesky_factors, walker_green):
    blk_count = lax.axis_size("blk")
    vec_count = lax.axis_size("vec")
    vectors, el, norb = cholesky_factors.shape
    vector_total = vectors * blk_count * vec_count
    groups = blk_count // 2
    assert vec_count == 4 and groups > 1 and groups & (groups - 1) == 0
    quarter = norb // vec_count
    bf, f32 = jnp.bfloat16, jnp.float32
    dma = pltpu.SemaphoreType.DMA
    gall = pl.pallas_call(
        functools.partial(gather_kernel, groups, vec_count),
        out_shape=jax.ShapeDtypeStruct((groups, 2, el, norb), bf),
        in_specs=[pl.BlockSpec(memory_space=pl.ANY)],
        out_specs=pl.BlockSpec(memory_space=pl.ANY),
        scratch_shapes=[dma] + [dma((groups,))] * 8 + [dma((groups, 2))] * 2,
        compiler_params=pltpu.CompilerParams(collective_id=0, has_side_effects=True),
        name="gather",
    )(walker_green)
    shared_portion = jnp.einsum(
        "gap,wbp->wgab",
        cholesky_factors,
        gall.reshape(blk_count, el, norb),
        preferred_element_type=f32,
    ).astype(bf)
    running = jnp.einsum(
        "vhlr,hrm->vlm", shared_portion, cholesky_factors, preferred_element_type=f32
    ).reshape(groups, 2, el, norb)
    gradient, energy = pl.pallas_call(
        functools.partial(
            reduce_kernel, groups, vec_count, -0.5 / (el * vector_total), 1.0 / math.sqrt(vector_total)
        ),
        out_shape=(
            jax.ShapeDtypeStruct((el, quarter), f32),
            jax.ShapeDtypeStruct((1,), f32),
        ),
        in_specs=[pl.BlockSpec(memory_space=pl.ANY)] * 2,
        out_specs=(
            pl.BlockSpec(memory_space=pltpu.VMEM),
            pl.BlockSpec(memory_space=pltpu.SMEM),
        ),
        scratch_shapes=[
            pltpu.VMEM((groups, 2, el, norb), f32),
            pltpu.VMEM((groups, el, quarter), bf),
            pltpu.VMEM((groups, 2, 2, el, quarter), bf),
            pltpu.VMEM((groups, 2, 2, el, quarter), bf),
            pltpu.VMEM((groups, 2, el, quarter), bf),
            pltpu.VMEM((groups, 2, el, quarter), bf),
            pltpu.VMEM((groups, el, quarter), bf),
            pltpu.VMEM((groups, el, quarter), bf),
            pltpu.VMEM((groups, el, quarter), f32),
            pltpu.VMEM((groups, el, quarter), bf),
            pltpu.VMEM((groups, el, quarter), bf),
            pltpu.VMEM((groups, vec_count, 8, 128), f32),
            pltpu.VMEM((groups, vec_count, 8, 128), f32),
            dma((groups,)), dma,
        ]
        + [dma((groups,))] * 4
        + [dma((groups, 2))] * 4
        + [dma((groups, vec_count))] * 2,
        compiler_params=pltpu.CompilerParams(
            collective_id=1, has_side_effects=True, vmem_limit_bytes=56 * 1024 * 1024
        ),
        name="reduce",
    )(running, gall)
    return gradient[None], energy


def solution(mesh):
    return jax.shard_map(
        shards,
        mesh=mesh,
        in_specs=(P(("blk", "vec"), None, None), P("blk", None, None)),
        out_specs=(P("blk", None, "vec"), P("blk")),
        check_vma=False,
    )
```

```python
import functools
import math

import jax
import jax.numpy as jnp
from jax import lax
from jax.experimental import pallas as pl
from jax.experimental.pallas import tpu as pltpu
from jax.sharding import PartitionSpec as P

MESH = pl.DeviceIdType.MESH


def flip(value, step, size):
    total, bit = 0, 1
    while bit < size:
        total = total + ((value // bit + step // bit) % 2) * bit
        bit *= 2
    return total


def kernel(
    groups, vec_count, energy_scale, grad_scale,
    l_hbm, g_hbm,
    grad_ref, energy_ref,
    l_ref, green, gall, inter, prod, core_out, core_in, x_out, x_in, own, y_out, y_in, kept, z_out, z_in, ebuf, e_in,
    l_sem, g_sem,
    gz_s, gz_r, gx_s, gx_r, gc0_s, gc0_r, gc1_s, gc1_r, ry_s, ry_r, rz_s, rz_r,
    gy_s, gy_r, rc_s, rc_r, rx_s, rx_r, e_s, e_r,
):
    blk, vec = lax.axis_index("blk"), lax.axis_index("vec")
    z, y = blk // 2, blk % 2
    x, c = vec // 2, vec % 2
    el = g_hbm.shape[1]
    norb = g_hbm.shape[2]
    vectors = l_hbm.shape[0]
    quarter = norb // vec_count
    half = norb // 2

    core_peer = {"blk": blk, "vec": x * 2 + (1 - c)}
    x_peer = {"blk": blk, "vec": (1 - x) * 2 + c}
    y_peer = {"blk": z * 2 + (1 - y), "vec": vec}

    def z_peer(k):
        return {"blk": flip(z, k, groups) * 2 + y, "vec": vec}

    def home(k, j):
        return {"blk": flip(z, k, groups) * 2 + y, "vec": flip(vec, j, vec_count)}

    mine = pl.ds(pl.multiple_of(c * half, half), half)
    part_me = pl.ds(pl.multiple_of(c * half + x * quarter, quarter), quarter)
    part_other = pl.ds(pl.multiple_of(c * half + (1 - x) * quarter, quarter), quarter)
    rows_me = pl.ds(pl.multiple_of(y * el, el), el)
    rows_other = pl.ds(pl.multiple_of((1 - y) * el, el), el)

    def remote(src, dst, s, r, peer):
        return pltpu.make_async_remote_copy(
            src_ref=src, dst_ref=dst, send_sem=s, recv_sem=r, device_id=peer, device_id_type=MESH
        )

    def gz(k):
        return remote(
            gall.at[0, y, part_me], gall.at[k, y, part_me], gz_s.at[k], gz_r.at[k], z_peer(k)
        )

    def gx(k):
        return remote(
            gall.at[k, y, part_me], gall.at[k, y, part_me], gx_s.at[k], gx_r.at[k], x_peer
        )

    def gy_first():
        return remote(
            gall.at[0, y, mine], gall.at[0, y, mine], gy_s.at[0, 0], gy_r.at[0, 0], y_peer
        )

    def gy(k, n):
        part = (part_me, part_other)[n]
        return remote(
            gall.at[k, y, part], gall.at[k, y, part], gy_s.at[k, n], gy_r.at[k, n], y_peer
        )

    def gc0(k):
        return remote(
            gall.at[k, y, mine], gall.at[k, y, mine], gc0_s.at[k], gc0_r.at[k], core_peer
        )

    def gc1(k):
        return remote(
            gall.at[k, 1 - y, mine], gall.at[k, 1 - y, mine], gc1_s.at[k], gc1_r.at[k], core_peer
        )

    def rc(k, part):
        return remote(
            core_out.at[k, part], core_in.at[k, part], rc_s.at[k, part], rc_r.at[k, part], core_peer
        )

    def rx(k, n):
        rows = (rows_other, rows_me)[n]
        return remote(
            x_out.at[k, rows], x_in.at[k, rows], rx_s.at[k, n], rx_r.at[k, n], x_peer
        )

    def ry(k):
        return remote(y_out.at[k], y_in.at[k], ry_s.at[k], ry_r.at[k], y_peer)

    def rz(k):
        return remote(z_out.at[k], z_in.at[k], rz_s.at[k], rz_r.at[k], z_peer(k))

    def energy_send(k, j):
        return remote(
            ebuf.at[k, vec], e_in.at[k, vec], e_s.at[k, j], e_r.at[k, j], home(k, j)
        )

    l_copy = pltpu.make_async_copy(l_hbm, l_ref, l_sem)
    g_copy = pltpu.make_async_copy(g_hbm.at[0], green, g_sem)
    g_copy.start()
    l_copy.start()

    barrier = pltpu.get_barrier_semaphore()
    pl.semaphore_signal(barrier, inc=1, device_id=y_peer, device_id_type=MESH)
    for k in range(groups):
        for j in range(vec_count):
            if k + j > 0:
                pl.semaphore_signal(barrier, inc=1, device_id=home(k, j), device_id_type=MESH)
    g_copy.wait()
    gall[0, y] = green[...].T
    pl.semaphore_wait(barrier, groups * vec_count)

    gy_first().start()
    for k in range(1, groups):
        gz(k).start()

    def first_service(k):
        gz(k).wait_recv()
        gx(k).start()
        gy(k, 0).start()

    def second_service(k):
        gx(k).wait_recv()
        gy(k, 1).start()
        gc0(k).start()

    def third_service(k):
        gy(k, 0).wait_recv()
        gy(k, 1).wait_recv()
        gc1(k).start()

    first_service(1)
    gy_first().wait_recv()
    gc1(0).start()
    second_service(1)
    if groups > 2:
        first_service(2)
    third_service(1)
    l_copy.wait()

    def columns(xq, cq):
        return pl.ds(pl.multiple_of((xq * 2 + cq) * quarter, quarter), quarter)

    def product(h, xq):
        cols = pl.ds(pl.multiple_of(xq * half, half), half)
        prod[...] = jnp.dot(
            inter[h * 2 * el : (h + 1) * 2 * el, :],
            l_ref[:, :, cols].reshape(vectors * el, half),
            preferred_element_type=jnp.float32,
        )

    def prod_part(cq):
        return prod[:, pl.ds(pl.multiple_of(cq * quarter, quarter), quarter)]

    def y_stage(k):
        rx(k, 0).wait_recv()
        y_out[k] = (
            own[k, rows_other, :] + x_in[k, rows_other, :].astype(jnp.float32)
        ).astype(jnp.bfloat16)
        ry(k).start()
        rx(k, 1).wait_recv()
        kept[k] = own[k, rows_me, :] + x_in[k, rows_me, :].astype(jnp.float32)

    def z_stage(k):
        ry(k).wait_recv()
        kept[k] = kept[k] + y_in[k].astype(jnp.float32)

        @pl.when(k > 0)
        def _():
            z_out[k] = kept[k].astype(jnp.bfloat16)
            rz(k).start()

        energy = jnp.sum(kept[k] * gall[k, y, columns(x, c)].astype(jnp.float32).T)
        ebuf[k, vec] = jnp.full(ebuf.shape[2:], energy, jnp.float32)
        for j in range(1, vec_count):
            energy_send(k, j).start()

        @pl.when(k > 0)
        def _():
            energy_send(k, 0).start()

    chunk = math.gcd(vectors, 4)

    def step(pair, carry):
        base = 2 * pair
        more = base + 2 < groups
        for h in range(2):
            gc1(base + h).wait_recv()
        gc0(base + 1).wait_recv()

        @pl.when(pair > 0)
        def _():
            gc0(base).wait_recv()

        @pl.when(more)
        def _():
            second_service(base + 2)
            first_service(base + 3)

        for first in range(0, vectors, chunk):
            block = lax.dot_general(
                l_ref[first : first + chunk].reshape(chunk * el, norb),
                jnp.concatenate([gall[base + w // 2, w % 2] for w in range(4)], axis=1),
                (((1,), (0,)), ((), ())),
                preferred_element_type=jnp.float32,
            ).astype(jnp.bfloat16)
            for g in range(chunk):
                for w in range(4):
                    inter[w * el : (w + 1) * el, (first + g) * el : (first + g + 1) * el] = block[
                        g * el : (g + 1) * el, w * el : (w + 1) * el
                    ]

        for h in range(2):
            k = base + h

            @pl.when(k > 1)
            def _():
                z_stage(k - 2)

            product(h, 1 - x)
            core_out[k, 0] = prod_part(1 - c).astype(jnp.bfloat16)
            rc(k, 0).start()
            own[k] = prod_part(c)
            product(h, x)
            core_out[k, 1] = prod_part(1 - c).astype(jnp.bfloat16)
            rc(k, 1).start()
            rc(k, 0).wait_recv()
            x_out[k] = (own[k] + core_in[k, 0].astype(jnp.float32)).astype(jnp.bfloat16)
            rx(k, 0).start()
            rx(k, 1).start()

            @pl.when(more)
            def _():
                if h == 0:
                    second_service(base + 3)
                    third_service(base + 2)
                else:
                    third_service(base + 3)

            if h == 1:

                @pl.when(base + 4 < groups)
                def _():
                    first_service(base + 4)

            rc(k, 1).wait_recv()
            own[k] = prod_part(c) + core_in[k, 1].astype(jnp.float32)

            @pl.when(k > 0)
            def _():
                y_stage(k - 1)

        return carry

    lax.fori_loop(0, groups // 2, step, 0)
    last = groups - 1
    y_stage(last)
    z_stage(last - 1)
    z_stage(last)

    total = kept[0]
    for k in range(1, groups):
        rz(k).wait_recv()
        total = total + z_in[k].astype(jnp.float32)
    grad_ref[...] = total * grad_scale

    e_in[0, vec] = ebuf[0, vec]
    for k in range(groups):
        for j in range(vec_count):
            if k + j > 0:
                energy_send(k, j).wait_recv()
    energies = jnp.zeros(e_in.shape[2:], jnp.float32)
    for k in range(groups):
        for n in range(vec_count):
            energies = energies + e_in[k, n]
    energy_ref[0] = jnp.max(energies) * energy_scale

    gy_first().wait_send()
    gc1(0).wait_send()
    for k in range(groups):
        for n in range(2):
            rc(k, n).wait_send()
            rx(k, n).wait_send()
        ry(k).wait_send()
        for j in range(vec_count):
            if k + j > 0:
                energy_send(k, j).wait_send()
        if k > 0:
            gz(k).wait_send()
            gx(k).wait_send()
            gy(k, 0).wait_send()
            gy(k, 1).wait_send()
            gc0(k).wait_send()
            gc1(k).wait_send()
            rz(k).wait_send()


def shards(cholesky_factors, walker_green):
    blk_count = lax.axis_size("blk")
    vec_count = lax.axis_size("vec")
    vectors, el, norb = cholesky_factors.shape
    vector_total = vectors * blk_count * vec_count
    groups = blk_count // 2
    assert vec_count == 4 and groups > 1 and groups & (groups - 1) == 0
    quarter = norb // vec_count
    bf, f32 = jnp.bfloat16, jnp.float32
    dma = pltpu.SemaphoreType.DMA
    flops = 4 * blk_count * vectors * el * el * norb
    gradient, energy = pl.pallas_call(
        functools.partial(
            kernel, groups, vec_count, -0.5 / (el * vector_total), 1.0 / math.sqrt(vector_total)
        ),
        out_shape=(
            jax.ShapeDtypeStruct((el, quarter), f32),
            jax.ShapeDtypeStruct((1,), f32),
        ),
        in_specs=[pl.BlockSpec(memory_space=pl.ANY)] * 2,
        out_specs=(
            pl.BlockSpec(memory_space=pltpu.VMEM),
            pl.BlockSpec(memory_space=pltpu.SMEM),
        ),
        scratch_shapes=[
            pltpu.VMEM((vectors, el, norb), bf),
            pltpu.VMEM((el, norb), bf),
            pltpu.VMEM((groups, 2, norb, el), bf),
            pltpu.VMEM((4 * el, vectors * el), bf),
            pltpu.VMEM((2 * el, norb // 2), f32),
            pltpu.VMEM((groups, 2, 2 * el, quarter), bf),
            pltpu.VMEM((groups, 2, 2 * el, quarter), bf),
            pltpu.VMEM((groups, 2 * el, quarter), bf),
            pltpu.VMEM((groups, 2 * el, quarter), bf),
            pltpu.VMEM((groups, 2 * el, quarter), f32),
            pltpu.VMEM((groups, el, quarter), bf),
            pltpu.VMEM((groups, el, quarter), bf),
            pltpu.VMEM((groups, el, quarter), f32),
            pltpu.VMEM((groups, el, quarter), bf),
            pltpu.VMEM((groups, el, quarter), bf),
            pltpu.VMEM((groups, vec_count, 8, 128), f32),
            pltpu.VMEM((groups, vec_count, 8, 128), f32),
            dma, dma,
        ]
        + [dma((groups,))] * 12
        + [dma((groups, 2))] * 6
        + [dma((groups, vec_count))] * 2,
        compiler_params=pltpu.CompilerParams(
            collective_id=0, has_side_effects=True, vmem_limit_bytes=56 * 1024 * 1024
        ),
        cost_estimate=pl.CostEstimate(
            flops=flops, bytes_accessed=2 * vectors * el * norb, transcendentals=0
        ),
        name="exchange",
    )(cholesky_factors, walker_green)
    return gradient[None], energy


def solution(mesh):
    return jax.shard_map(
        shards,
        mesh=mesh,
        in_specs=(P(("blk", "vec"), None, None), P("blk", None, None)),
        out_specs=(P("blk", None, "vec"), P("blk")),
        check_vma=False,
    )
```

```python
import functools
import math

import jax
import jax.numpy as jnp
from jax import lax
from jax.experimental import pallas as pl
from jax.experimental.pallas import tpu as pltpu
from jax.sharding import PartitionSpec as P

MESH = pl.DeviceIdType.MESH


def flip(value, step, size):
    total, bit = 0, 1
    while bit < size:
        total = total + ((value // bit + step // bit) % 2) * bit
        bit *= 2
    return total


def kernel(
    groups, vec_count, energy_scale, grad_scale,
    l_hbm, g_hbm,
    grad_ref, energy_ref,
    l_ref, green, gall, inter, prod, core_out, core_in, a1_out, a1_in, b1_out, b1_in, own, a2_out, a2_in, b2_out, b2_in, kept, z_out, z_in, ebuf, e_in,
    l_sem, g_sem,
    gz_s, gz_r, gx_s, gx_r, gc0_s, gc0_r, gc1_s, gc1_r, rz_s, rz_r,
    gy_s, gy_r, rc_s, rc_r, rx_s, rx_r, ry_s, ry_r, e_s, e_r,
):
    blk, vec = lax.axis_index("blk"), lax.axis_index("vec")
    z, y = blk // 2, blk % 2
    x, c = vec // 2, vec % 2
    el = g_hbm.shape[1]
    norb = g_hbm.shape[2]
    vectors = l_hbm.shape[0]
    quarter = norb // vec_count
    half = norb // 2

    core_peer = {"blk": blk, "vec": x * 2 + (1 - c)}
    x_peer = {"blk": blk, "vec": (1 - x) * 2 + c}
    y_peer = {"blk": z * 2 + (1 - y), "vec": vec}

    def z_peer(k):
        return {"blk": flip(z, k, groups) * 2 + y, "vec": vec}

    def home(k, j):
        return {"blk": flip(z, k, groups) * 2 + y, "vec": flip(vec, j, vec_count)}

    mine = pl.ds(pl.multiple_of(c * half, half), half)
    part_me = pl.ds(pl.multiple_of(c * half + x * quarter, quarter), quarter)
    part_other = pl.ds(pl.multiple_of(c * half + (1 - x) * quarter, quarter), quarter)
    rows_me = pl.ds(pl.multiple_of(y * el, el), el)
    rows_other = pl.ds(pl.multiple_of((1 - y) * el, el), el)

    def remote(src, dst, s, r, peer):
        return pltpu.make_async_remote_copy(
            src_ref=src, dst_ref=dst, send_sem=s, recv_sem=r, device_id=peer, device_id_type=MESH
        )

    def gz(k):
        return remote(
            gall.at[0, y, part_me], gall.at[k, y, part_me], gz_s.at[k], gz_r.at[k], z_peer(k)
        )

    def gx(k):
        return remote(
            gall.at[k, y, part_me], gall.at[k, y, part_me], gx_s.at[k], gx_r.at[k], x_peer
        )

    def gy_first():
        return remote(
            gall.at[0, y, mine], gall.at[0, y, mine], gy_s.at[0, 0], gy_r.at[0, 0], y_peer
        )

    def gy(k, n):
        part = (part_me, part_other)[n]
        return remote(
            gall.at[k, y, part], gall.at[k, y, part], gy_s.at[k, n], gy_r.at[k, n], y_peer
        )

    def gx_other(k):
        view = gall.at[k, 1 - y, part_me]
        return remote(view, view, gy_s.at[k, 1], gy_r.at[k, 1], x_peer)

    def gc0(k):
        return remote(
            gall.at[k, y, mine], gall.at[k, y, mine], gc0_s.at[k], gc0_r.at[k], core_peer
        )

    def gc1(k):
        return remote(
            gall.at[k, 1 - y, mine], gall.at[k, 1 - y, mine], gc1_s.at[k], gc1_r.at[k], core_peer
        )

    def rc(k, part):
        return remote(
            core_out.at[k, part], core_in.at[k, part], rc_s.at[k, part], rc_r.at[k, part], core_peer
        )

    def rx(k, n):
        out, into = ((a1_out, a1_in), (b2_out, b2_in))[n]
        return remote(out.at[k], into.at[k], rx_s.at[k, n], rx_r.at[k, n], x_peer)

    def ry(k, n):
        out, into = ((b1_out, b1_in), (a2_out, a2_in))[n]
        return remote(out.at[k], into.at[k], ry_s.at[k, n], ry_r.at[k, n], y_peer)

    def rz(k):
        return remote(z_out.at[k], z_in.at[k], rz_s.at[k], rz_r.at[k], z_peer(k))

    def energy_send(k, j):
        return remote(
            ebuf.at[k, vec], e_in.at[k, vec], e_s.at[k, j], e_r.at[k, j], home(k, j)
        )

    l_copy = pltpu.make_async_copy(l_hbm, l_ref, l_sem)
    g_copy = pltpu.make_async_copy(g_hbm.at[0], green, g_sem)
    g_copy.start()
    l_copy.start()

    barrier = pltpu.get_barrier_semaphore()
    pl.semaphore_signal(barrier, inc=1, device_id=y_peer, device_id_type=MESH)
    for k in range(groups):
        for j in range(vec_count):
            if k + j > 0:
                pl.semaphore_signal(barrier, inc=1, device_id=home(k, j), device_id_type=MESH)
    g_copy.wait()
    gall[0, y] = green[...].T
    pl.semaphore_wait(barrier, groups * vec_count)

    gy_first().start()
    for k in range(1, groups):
        gz(k).start()

    def first_service(k):
        gz(k).wait_recv()
        gx(k).start()
        gy(k, 0).start()

    def second_service(k, odd):
        gx(k).wait_recv()
        gc0(k).start()
        if odd:
            gy(k, 0).wait_recv()
            gx_other(k).start()
        else:
            gy(k, 1).start()

    def third_service(k, odd):
        if odd:
            gx_other(k).wait_recv()
        else:
            gy(k, 0).wait_recv()
            gy(k, 1).wait_recv()
        gc1(k).start()

    first_service(1)
    gy_first().wait_recv()
    gc1(0).start()
    second_service(1, True)
    if groups > 2:
        first_service(2)
    third_service(1, True)
    l_copy.wait()

    def columns(xq, cq):
        return pl.ds(pl.multiple_of((xq * 2 + cq) * quarter, quarter), quarter)

    def product(xq):
        cols = pl.ds(pl.multiple_of(xq * half, half), half)
        prod[...] = jnp.dot(
            inter[...],
            l_ref[:, :, cols].reshape(vectors * el, half),
            preferred_element_type=jnp.float32,
        )

    def prod_part(h, cq):
        return prod[
            h * 2 * el : (h + 1) * 2 * el, pl.ds(pl.multiple_of(cq * quarter, quarter), quarter)
        ]

    f32, bf = jnp.float32, jnp.bfloat16
    hq = quarter // 2

    def y_stage(k):
        rx(k, 0).wait_recv()
        a2_out[k] = (own[k, 1, rows_other, :hq] + a1_in[k, rows_other].astype(f32)).astype(bf)
        ry(k, 1).start()
        ry(k, 0).wait_recv()
        b2_out[k] = (own[k, 0, rows_me, hq:] + b1_in[k, 0].astype(f32)).astype(bf)
        rx(k, 1).start()
        kept[k, :, :hq] = own[k, 1, rows_me, :hq] + a1_in[k, rows_me].astype(f32)
        kept[k, :, hq:] = own[k, 1, rows_me, hq:] + b1_in[k, 1].astype(f32)

    def z_stage(k):
        ry(k, 1).wait_recv()
        kept[k, :, :hq] += a2_in[k].astype(f32)
        rx(k, 1).wait_recv()
        kept[k, :, hq:] += b2_in[k].astype(f32)

        @pl.when(k > 0)
        def _():
            z_out[k] = kept[k].astype(jnp.bfloat16)
            rz(k).start()

        energy = jnp.sum(kept[k] * gall[k, y, columns(x, c)].astype(jnp.float32).T)
        ebuf[k, vec] = jnp.full(ebuf.shape[2:], energy, jnp.float32)
        for j in range(1, vec_count):
            energy_send(k, j).start()

        @pl.when(k > 0)
        def _():
            energy_send(k, 0).start()

    chunk = vectors

    def step(pair, carry):
        base = 2 * pair
        more = base + 2 < groups
        for h in range(2):
            gc1(base + h).wait_recv()
        gc0(base + 1).wait_recv()

        @pl.when(pair > 0)
        def _():
            gc0(base).wait_recv()

        @pl.when(more)
        def _():
            second_service(base + 2, False)
            first_service(base + 3)

        for first in range(0, vectors, chunk):
            block = lax.dot_general(
                l_ref[first : first + chunk].reshape(chunk * el, norb),
                jnp.concatenate([gall[base + w // 2, w % 2] for w in range(4)], axis=1),
                (((1,), (0,)), ((), ())),
                preferred_element_type=jnp.float32,
            ).astype(jnp.bfloat16)
            for g in range(chunk):
                for w in range(4):
                    inter[w * el : (w + 1) * el, (first + g) * el : (first + g + 1) * el] = block[
                        g * el : (g + 1) * el, w * el : (w + 1) * el
                    ]

        for h in range(2):

            @pl.when(pair > 0)
            def _():
                y_stage(base + h - 2)

        product(1 - x)
        for h in range(2):
            k = base + h
            core_out[k, 0] = prod_part(h, 1 - c).astype(bf)
            rc(k, 0).start()
            own[k, 0] = prod_part(h, c)

        @pl.when(more)
        def _():
            second_service(base + 3, True)
            third_service(base + 2, False)

        product(x)
        for h in range(2):
            k = base + h
            core_out[k, 1] = prod_part(h, 1 - c).astype(bf)
            rc(k, 1).start()
        for h in range(2):
            k = base + h
            rc(k, 0).wait_recv()
            own[k, 0] += core_in[k, 0].astype(f32)
            a1_out[k] = own[k, 0, :, :hq].astype(bf)
            rx(k, 0).start()
        for h in range(2):
            k = base + h
            rc(k, 1).wait_recv()
            own[k, 1] = prod_part(h, c) + core_in[k, 1].astype(f32)
            for n in range(2):
                b1_out[k, n] = own[k, n, rows_other, hq:].astype(bf)
            ry(k, 0).start()

        @pl.when(more)
        def _():
            third_service(base + 3, True)

        @pl.when(base + 4 < groups)
        def _():
            first_service(base + 4)

        @pl.when(pair > 0)
        def _():
            z_stage(base - 2)
            z_stage(base - 1)

        return carry

    lax.fori_loop(0, groups // 2, step, 0)
    last = groups - 1
    y_stage(last - 1)
    y_stage(last)
    z_stage(last - 1)
    z_stage(last)

    total = kept[0]
    for k in range(1, groups):
        rz(k).wait_recv()
        total = total + z_in[k].astype(jnp.float32)
    grad_ref[...] = total * grad_scale

    e_in[0, vec] = ebuf[0, vec]
    for k in range(groups):
        for j in range(vec_count):
            if k + j > 0:
                energy_send(k, j).wait_recv()
    energies = jnp.zeros(e_in.shape[2:], jnp.float32)
    for k in range(groups):
        for n in range(vec_count):
            energies = energies + e_in[k, n]
    energy_ref[0] = jnp.max(energies) * energy_scale

    gy_first().wait_send()
    gc1(0).wait_send()
    for k in range(groups):
        for n in range(2):
            rc(k, n).wait_send()
            rx(k, n).wait_send()
            ry(k, n).wait_send()
        for j in range(vec_count):
            if k + j > 0:
                energy_send(k, j).wait_send()
        if k > 0:
            gz(k).wait_send()
            gx(k).wait_send()
            gy(k, 0).wait_send()
            (gx_other(k) if k % 2 else gy(k, 1)).wait_send()
            gc0(k).wait_send()
            gc1(k).wait_send()
            rz(k).wait_send()


def shards(cholesky_factors, walker_green):
    blk_count = lax.axis_size("blk")
    vec_count = lax.axis_size("vec")
    vectors, el, norb = cholesky_factors.shape
    vector_total = vectors * blk_count * vec_count
    groups = blk_count // 2
    assert vec_count == 4 and groups > 1 and groups & (groups - 1) == 0
    quarter = norb // vec_count
    hq = quarter // 2
    bf, f32 = jnp.bfloat16, jnp.float32
    dma = pltpu.SemaphoreType.DMA
    flops = 4 * blk_count * vectors * el * el * norb
    gradient, energy = pl.pallas_call(
        functools.partial(
            kernel, groups, vec_count, -0.5 / (el * vector_total), 1.0 / math.sqrt(vector_total)
        ),
        out_shape=(
            jax.ShapeDtypeStruct((el, quarter), f32),
            jax.ShapeDtypeStruct((1,), f32),
        ),
        in_specs=[pl.BlockSpec(memory_space=pl.ANY)] * 2,
        out_specs=(
            pl.BlockSpec(memory_space=pltpu.VMEM),
            pl.BlockSpec(memory_space=pltpu.SMEM),
        ),
        scratch_shapes=[
            pltpu.VMEM((vectors, el, norb), bf),
            pltpu.VMEM((el, norb), bf),
            pltpu.VMEM((groups, 2, norb, el), bf),
            pltpu.VMEM((4 * el, vectors * el), bf),
            pltpu.VMEM((4 * el, norb // 2), f32),
            pltpu.VMEM((groups, 2, 2 * el, quarter), bf),
            pltpu.VMEM((groups, 2, 2 * el, quarter), bf),
            pltpu.VMEM((groups, 2 * el, hq), bf),
            pltpu.VMEM((groups, 2 * el, hq), bf),
            pltpu.VMEM((groups, 2, el, hq), bf),
            pltpu.VMEM((groups, 2, el, hq), bf),
            pltpu.VMEM((groups, 2, 2 * el, quarter), f32),
            pltpu.VMEM((groups, el, hq), bf),
            pltpu.VMEM((groups, el, hq), bf),
            pltpu.VMEM((groups, el, hq), bf),
            pltpu.VMEM((groups, el, hq), bf),
            pltpu.VMEM((groups, el, quarter), f32),
            pltpu.VMEM((groups, el, quarter), bf),
            pltpu.VMEM((groups, el, quarter), bf),
            pltpu.VMEM((groups, vec_count, 8, 128), f32),
            pltpu.VMEM((groups, vec_count, 8, 128), f32),
            dma, dma,
        ]
        + [dma((groups,))] * 10
        + [dma((groups, 2))] * 8
        + [dma((groups, vec_count))] * 2,
        compiler_params=pltpu.CompilerParams(
            collective_id=0, has_side_effects=True, vmem_limit_bytes=56 * 1024 * 1024
        ),
        cost_estimate=pl.CostEstimate(
            flops=flops, bytes_accessed=2 * vectors * el * norb, transcendentals=0
        ),
        name="exchange",
    )(cholesky_factors, walker_green)
    return gradient[None], energy


def solution(mesh):
    return jax.shard_map(
        shards,
        mesh=mesh,
        in_specs=(P(("blk", "vec"), None, None), P("blk", None, None)),
        out_specs=(P("blk", None, "vec"), P("blk")),
        check_vma=False,
    )
```

```python
import functools
import math

import jax
import jax.numpy as jnp
from jax import lax
from jax.experimental import pallas as pl
from jax.experimental.pallas import tpu as pltpu
from jax.sharding import PartitionSpec as P

MESH = pl.DeviceIdType.MESH


def flip(value, step, size):
    total, bit = 0, 1
    while bit < size:
        total = total + ((value // bit + step // bit) % 2) * bit
        bit *= 2
    return total


def kernel(
    groups, vec_count, energy_scale, grad_scale,
    l_hbm, g_hbm,
    grad_ref, energy_ref,
    l_ref, green, gall, inter, prod, core_out, core_in, a1_out, a1_in, b1_out, b1_in, own, a2_out, a2_in, b2_out, b2_in, kept, z_out, z_in, ebuf, e_in,
    l_sem, g_sem,
    gz_s, gz_r, gx_s, gx_r, gc0_s, gc0_r, gc1_s, gc1_r, rz_s, rz_r,
    gy_s, gy_r, rc_s, rc_r, rx_s, rx_r, ry_s, ry_r, e_s, e_r,
):
    blk, vec = lax.axis_index("blk"), lax.axis_index("vec")
    z, y = blk // 2, blk % 2
    x, c = vec // 2, vec % 2
    el = g_hbm.shape[1]
    norb = g_hbm.shape[2]
    vectors = l_hbm.shape[0]
    quarter = norb // vec_count
    half = norb // 2

    core_peer = {"blk": blk, "vec": x * 2 + (1 - c)}
    x_peer = {"blk": blk, "vec": (1 - x) * 2 + c}
    y_peer = {"blk": z * 2 + (1 - y), "vec": vec}

    def z_peer(k):
        return {"blk": flip(z, k, groups) * 2 + y, "vec": vec}

    def home(k, j):
        return {"blk": flip(z, k, groups) * 2 + y, "vec": flip(vec, j, vec_count)}

    mine = pl.ds(pl.multiple_of(c * half, half), half)
    part_me = pl.ds(pl.multiple_of(c * half + x * quarter, quarter), quarter)
    part_other = pl.ds(pl.multiple_of(c * half + (1 - x) * quarter, quarter), quarter)
    rows_me = pl.ds(pl.multiple_of(y * el, el), el)
    rows_other = pl.ds(pl.multiple_of((1 - y) * el, el), el)

    def remote(src, dst, s, r, peer):
        return pltpu.make_async_remote_copy(
            src_ref=src, dst_ref=dst, send_sem=s, recv_sem=r, device_id=peer, device_id_type=MESH
        )

    def gz(k):
        return remote(
            gall.at[0, y, part_me], gall.at[k, y, part_me], gz_s.at[k], gz_r.at[k], z_peer(k)
        )

    def gx(k):
        return remote(
            gall.at[k, y, part_me], gall.at[k, y, part_me], gx_s.at[k], gx_r.at[k], x_peer
        )

    def gy_first():
        return remote(
            gall.at[0, y, mine], gall.at[0, y, mine], gy_s.at[0, 0], gy_r.at[0, 0], y_peer
        )

    def gy(k, n):
        part = (part_me, part_other)[n]
        return remote(
            gall.at[k, y, part], gall.at[k, y, part], gy_s.at[k, n], gy_r.at[k, n], y_peer
        )

    def gx_other(k):
        view = gall.at[k, 1 - y, part_me]
        return remote(view, view, gy_s.at[k, 1], gy_r.at[k, 1], x_peer)

    def gc0(k):
        return remote(
            gall.at[k, y, mine], gall.at[k, y, mine], gc0_s.at[k], gc0_r.at[k], core_peer
        )

    def gc1(k):
        return remote(
            gall.at[k, 1 - y, mine], gall.at[k, 1 - y, mine], gc1_s.at[k], gc1_r.at[k], core_peer
        )

    def rc(k, part):
        return remote(
            core_out.at[k, part], core_in.at[k, part], rc_s.at[k, part], rc_r.at[k, part], core_peer
        )

    def rx(k, n):
        out, into = ((a1_out, a1_in), (b2_out, b2_in))[n]
        return remote(out.at[k], into.at[k], rx_s.at[k, n], rx_r.at[k, n], x_peer)

    def ry(k, n):
        out, into = ((b1_out, b1_in), (a2_out, a2_in))[n]
        return remote(out.at[k], into.at[k], ry_s.at[k, n], ry_r.at[k, n], y_peer)

    def rz(k):
        return remote(z_out.at[k], z_in.at[k], rz_s.at[k], rz_r.at[k], z_peer(k))

    def energy_send(k, j):
        return remote(
            ebuf.at[k, vec], e_in.at[k, vec], e_s.at[k, j], e_r.at[k, j], home(k, j)
        )

    l_copy = pltpu.make_async_copy(l_hbm, l_ref, l_sem)
    g_copy = pltpu.make_async_copy(g_hbm.at[0], green, g_sem)
    g_copy.start()
    l_copy.start()

    barrier = pltpu.get_barrier_semaphore()
    pl.semaphore_signal(barrier, inc=1, device_id=y_peer, device_id_type=MESH)
    for k in range(groups):
        for j in range(vec_count):
            if k + j > 0:
                pl.semaphore_signal(barrier, inc=1, device_id=home(k, j), device_id_type=MESH)
    g_copy.wait()
    gall[0, y] = green[...].T
    pl.semaphore_wait(barrier, groups * vec_count)

    for k in range(1, groups):
        gz(k).start()

    def first_service(k):
        gz(k).wait_recv()
        gx(k).start()
        gy(k, 0).start()

    def second_service(k, odd):
        gx(k).wait_recv()
        gc0(k).start()
        if odd:
            gy(k, 0).wait_recv()
            gx_other(k).start()
        else:
            gy(k, 1).start()

    def third_service(k, odd):
        if odd:
            gx_other(k).wait_recv()
        else:
            gy(k, 0).wait_recv()
            gy(k, 1).wait_recv()
        gc1(k).start()

    first_service(1)
    if groups > 2:
        first_service(2)
    gy_first().start()
    second_service(1, True)
    if groups > 2:
        second_service(2, False)
        first_service(3)
    third_service(1, True)
    if groups > 2:
        third_service(2, False)
    gy_first().wait_recv()
    gc1(0).start()
    l_copy.wait()

    def columns(xq, cq):
        return pl.ds(pl.multiple_of((xq * 2 + cq) * quarter, quarter), quarter)

    def product(xq):
        cols = pl.ds(pl.multiple_of(xq * half, half), half)
        prod[...] = jnp.dot(
            inter[...],
            l_ref[:, :, cols].reshape(vectors * el, half),
            preferred_element_type=jnp.float32,
        )

    def prod_part(h, cq):
        return prod[
            h * 2 * el : (h + 1) * 2 * el, pl.ds(pl.multiple_of(cq * quarter, quarter), quarter)
        ]

    f32, bf = jnp.float32, jnp.bfloat16
    hq = quarter // 2

    def y_stage(k):
        rx(k, 0).wait_recv()
        a2_out[k] = (own[k, 1, rows_other, :hq] + a1_in[k, rows_other].astype(f32)).astype(bf)
        ry(k, 1).start()
        ry(k, 0).wait_recv()
        b2_out[k] = (own[k, 0, rows_me, hq:] + b1_in[k, 0].astype(f32)).astype(bf)
        rx(k, 1).start()
        kept[k, :, :hq] = own[k, 1, rows_me, :hq] + a1_in[k, rows_me].astype(f32)
        kept[k, :, hq:] = own[k, 1, rows_me, hq:] + b1_in[k, 1].astype(f32)

    def z_stage(k):
        ry(k, 1).wait_recv()
        kept[k, :, :hq] += a2_in[k].astype(f32)
        rx(k, 1).wait_recv()
        kept[k, :, hq:] += b2_in[k].astype(f32)

        @pl.when(k > 0)
        def _():
            z_out[k] = kept[k].astype(jnp.bfloat16)
            rz(k).start()

        energy = jnp.sum(kept[k] * gall[k, y, columns(x, c)].astype(jnp.float32).T)
        ebuf[k, vec] = jnp.full(ebuf.shape[2:], energy, jnp.float32)
        for j in range(1, vec_count):
            energy_send(k, j).start()

        @pl.when(k > 0)
        def _():
            energy_send(k, 0).start()

    chunk = vectors

    def step(pair, carry):
        base = 2 * pair
        more = base + 2 < groups
        after = base + 4 < groups
        ks = (base + 1, lax.rem(base + 2, groups))
        for k in ks:
            gc1(k).wait_recv()
        gc0(ks[0]).wait_recv()

        @pl.when(more)
        def _():
            gc0(ks[1]).wait_recv()
            second_service(base + 3, True)

        @pl.when(after)
        def _():
            first_service(base + 4)

        for first in range(0, vectors, chunk):
            block = lax.dot_general(
                l_ref[first : first + chunk].reshape(chunk * el, norb),
                jnp.concatenate([gall[ks[w // 2], w % 2] for w in range(4)], axis=1),
                (((1,), (0,)), ((), ())),
                preferred_element_type=jnp.float32,
            ).astype(jnp.bfloat16)
            for g in range(chunk):
                for w in range(4):
                    inter[w * el : (w + 1) * el, (first + g) * el : (first + g + 1) * el] = block[
                        g * el : (g + 1) * el, w * el : (w + 1) * el
                    ]

        for h in range(2):

            @pl.when(pair > 0)
            def _():
                y_stage(base + h - 1)

        product(1 - x)
        for h in range(2):
            k = ks[h]
            core_out[k, 0] = prod_part(h, 1 - c).astype(bf)
            rc(k, 0).start()
            own[k, 0] = prod_part(h, c)

        @pl.when(more)
        def _():
            third_service(base + 3, True)

        @pl.when(after)
        def _():
            second_service(base + 4, False)

        product(x)
        for h in range(2):
            k = ks[h]
            core_out[k, 1] = prod_part(h, 1 - c).astype(bf)
            rc(k, 1).start()
        for h in range(2):
            k = ks[h]
            rc(k, 0).wait_recv()
            own[k, 0] += core_in[k, 0].astype(f32)
            a1_out[k] = own[k, 0, :, :hq].astype(bf)
            rx(k, 0).start()
        for h in range(2):
            k = ks[h]
            rc(k, 1).wait_recv()
            own[k, 1] = prod_part(h, c) + core_in[k, 1].astype(f32)
            for n in range(2):
                b1_out[k, n] = own[k, n, rows_other, hq:].astype(bf)
            ry(k, 0).start()

        @pl.when(after)
        def _():
            third_service(base + 4, False)
            first_service(base + 5)

        @pl.when(pair > 0)
        def _():
            z_stage(base - 1)
            z_stage(base)

        return carry

    lax.fori_loop(0, groups // 2, step, 0)
    last = groups - 1
    y_stage(last)
    y_stage(0)
    z_stage(last)
    z_stage(0)

    total = kept[0]
    for k in range(1, groups):
        rz(k).wait_recv()
        total = total + z_in[k].astype(jnp.float32)
    grad_ref[...] = total * grad_scale

    e_in[0, vec] = ebuf[0, vec]
    for k in range(groups):
        for j in range(vec_count):
            if k + j > 0:
                energy_send(k, j).wait_recv()
    energies = jnp.zeros(e_in.shape[2:], jnp.float32)
    for k in range(groups):
        for n in range(vec_count):
            energies = energies + e_in[k, n]
    energy_ref[0] = jnp.max(energies) * energy_scale

    gy_first().wait_send()
    gc1(0).wait_send()
    for k in range(groups):
        for n in range(2):
            rc(k, n).wait_send()
            rx(k, n).wait_send()
            ry(k, n).wait_send()
        for j in range(vec_count):
            if k + j > 0:
                energy_send(k, j).wait_send()
        if k > 0:
            gz(k).wait_send()
            gx(k).wait_send()
            gy(k, 0).wait_send()
            (gx_other(k) if k % 2 else gy(k, 1)).wait_send()
            gc0(k).wait_send()
            gc1(k).wait_send()
            rz(k).wait_send()


def shards(cholesky_factors, walker_green):
    blk_count = lax.axis_size("blk")
    vec_count = lax.axis_size("vec")
    vectors, el, norb = cholesky_factors.shape
    vector_total = vectors * blk_count * vec_count
    groups = blk_count // 2
    assert vec_count == 4 and groups > 1 and groups & (groups - 1) == 0
    quarter = norb // vec_count
    hq = quarter // 2
    bf, f32 = jnp.bfloat16, jnp.float32
    dma = pltpu.SemaphoreType.DMA
    flops = 4 * blk_count * vectors * el * el * norb
    gradient, energy = pl.pallas_call(
        functools.partial(
            kernel, groups, vec_count, -0.5 / (el * vector_total), 1.0 / math.sqrt(vector_total)
        ),
        out_shape=(
            jax.ShapeDtypeStruct((el, quarter), f32),
            jax.ShapeDtypeStruct((1,), f32),
        ),
        in_specs=[pl.BlockSpec(memory_space=pl.ANY)] * 2,
        out_specs=(
            pl.BlockSpec(memory_space=pltpu.VMEM),
            pl.BlockSpec(memory_space=pltpu.SMEM),
        ),
        scratch_shapes=[
            pltpu.VMEM((vectors, el, norb), bf),
            pltpu.VMEM((el, norb), bf),
            pltpu.VMEM((groups, 2, norb, el), bf),
            pltpu.VMEM((4 * el, vectors * el), bf),
            pltpu.VMEM((4 * el, norb // 2), f32),
            pltpu.VMEM((groups, 2, 2 * el, quarter), bf),
            pltpu.VMEM((groups, 2, 2 * el, quarter), bf),
            pltpu.VMEM((groups, 2 * el, hq), bf),
            pltpu.VMEM((groups, 2 * el, hq), bf),
            pltpu.VMEM((groups, 2, el, hq), bf),
            pltpu.VMEM((groups, 2, el, hq), bf),
            pltpu.VMEM((groups, 2, 2 * el, quarter), f32),
            pltpu.VMEM((groups, el, hq), bf),
            pltpu.VMEM((groups, el, hq), bf),
            pltpu.VMEM((groups, el, hq), bf),
            pltpu.VMEM((groups, el, hq), bf),
            pltpu.VMEM((groups, el, quarter), f32),
            pltpu.VMEM((groups, el, quarter), bf),
            pltpu.VMEM((groups, el, quarter), bf),
            pltpu.VMEM((groups, vec_count, 8, 128), f32),
            pltpu.VMEM((groups, vec_count, 8, 128), f32),
            dma, dma,
        ]
        + [dma((groups,))] * 10
        + [dma((groups, 2))] * 8
        + [dma((groups, vec_count))] * 2,
        compiler_params=pltpu.CompilerParams(
            collective_id=0, has_side_effects=True, vmem_limit_bytes=56 * 1024 * 1024
        ),
        cost_estimate=pl.CostEstimate(
            flops=flops, bytes_accessed=2 * vectors * el * norb, transcendentals=0
        ),
        name="exchange",
    )(cholesky_factors, walker_green)
    return gradient[None], energy


def solution(mesh):
    return jax.shard_map(
        shards,
        mesh=mesh,
        in_specs=(P(("blk", "vec"), None, None), P("blk", None, None)),
        out_specs=(P("blk", None, "vec"), P("blk")),
        check_vma=False,
    )
```

```python
import functools
import math

import jax
import jax.numpy as jnp
from jax import lax
from jax.experimental import pallas as pl
from jax.experimental.pallas import tpu as pltpu
from jax.sharding import PartitionSpec as P

MESH = pl.DeviceIdType.MESH


def flip(value, step, size):
    total, bit = 0, 1
    while bit < size:
        total = total + ((value // bit + step // bit) % 2) * bit
        bit *= 2
    return total


def kernel(
    groups, vec_count, energy_scale, grad_scale,
    l_hbm, g_hbm,
    grad_ref, energy_ref,
    l_ref, green, gall, inter, prod, core_out, core_in, a1_out, a1_in, b1_out, b1_in, own, a2_out, a2_in, b2_out, b2_in, kept, z_out, z_in, ebuf, e_in,
    l_sem, g_sem,
    gz_s, gz_r, gx_s, gx_r, gc0_s, gc0_r, gc1_s, gc1_r, rz_s, rz_r,
    gy_s, gy_r, rc_s, rc_r, rx_s, rx_r, ry_s, ry_r, e_s, e_r,
):
    blk, vec = lax.axis_index("blk"), lax.axis_index("vec")
    z, y = blk // 2, blk % 2
    x, c = vec // 2, vec % 2
    el = g_hbm.shape[1]
    norb = g_hbm.shape[2]
    vectors = l_hbm.shape[0]
    quarter = norb // vec_count
    half = norb // 2

    core_peer = {"blk": blk, "vec": x * 2 + (1 - c)}
    x_peer = {"blk": blk, "vec": (1 - x) * 2 + c}
    y_peer = {"blk": z * 2 + (1 - y), "vec": vec}

    def z_peer(k):
        return {"blk": flip(z, k, groups) * 2 + y, "vec": vec}

    def home(k, j):
        return {"blk": flip(z, k, groups) * 2 + y, "vec": flip(vec, j, vec_count)}

    mine = pl.ds(pl.multiple_of(c * half, half), half)
    part_me = pl.ds(pl.multiple_of(c * half + x * quarter, quarter), quarter)
    part_other = pl.ds(pl.multiple_of(c * half + (1 - x) * quarter, quarter), quarter)
    rows_me = pl.ds(pl.multiple_of(y * el, el), el)
    rows_other = pl.ds(pl.multiple_of((1 - y) * el, el), el)

    def remote(src, dst, s, r, peer):
        return pltpu.make_async_remote_copy(
            src_ref=src, dst_ref=dst, send_sem=s, recv_sem=r, device_id=peer, device_id_type=MESH
        )

    def gz(k):
        return remote(
            gall.at[0, y, part_me], gall.at[k, y, part_me], gz_s.at[k], gz_r.at[k], z_peer(k)
        )

    def gx(k):
        return remote(
            gall.at[k, y, part_me], gall.at[k, y, part_me], gx_s.at[k], gx_r.at[k], x_peer
        )

    def gy_first():
        return remote(
            gall.at[0, y, mine], gall.at[0, y, mine], gy_s.at[0, 0], gy_r.at[0, 0], y_peer
        )

    def gy(k, n):
        part = (part_me, part_other)[n]
        return remote(
            gall.at[k, y, part], gall.at[k, y, part], gy_s.at[k, n], gy_r.at[k, n], y_peer
        )

    def gx_other(k):
        view = gall.at[k, 1 - y, part_me]
        return remote(view, view, gy_s.at[k, 1], gy_r.at[k, 1], x_peer)

    def gc0(k):
        return remote(
            gall.at[k, y, mine], gall.at[k, y, mine], gc0_s.at[k], gc0_r.at[k], core_peer
        )

    def gc1(k):
        return remote(
            gall.at[k, 1 - y, mine], gall.at[k, 1 - y, mine], gc1_s.at[k], gc1_r.at[k], core_peer
        )

    def rc(k, part):
        return remote(
            core_out.at[k, part], core_in.at[k, part], rc_s.at[k, part], rc_r.at[k, part], core_peer
        )

    def rx(k, n):
        out, into = ((a1_out, a1_in), (b2_out, b2_in))[n]
        return remote(out.at[k], into.at[k], rx_s.at[k, n], rx_r.at[k, n], x_peer)

    def ry(k, n):
        out, into = ((b1_out, b1_in), (a2_out, a2_in))[n]
        return remote(out.at[k], into.at[k], ry_s.at[k, n], ry_r.at[k, n], y_peer)

    def rz(k):
        return remote(z_out.at[k], z_in.at[k], rz_s.at[k], rz_r.at[k], z_peer(k))

    def energy_send(k, j):
        return remote(
            ebuf.at[k, vec], e_in.at[k, vec], e_s.at[k, j], e_r.at[k, j], home(k, j)
        )

    l_copy = pltpu.make_async_copy(l_hbm, l_ref, l_sem)
    g_copy = pltpu.make_async_copy(g_hbm.at[0], green, g_sem)
    g_copy.start()
    l_copy.start()

    barrier = pltpu.get_barrier_semaphore()
    pl.semaphore_signal(barrier, inc=1, device_id=y_peer, device_id_type=MESH)
    for k in range(groups):
        for j in range(vec_count):
            if k + j > 0:
                pl.semaphore_signal(barrier, inc=1, device_id=home(k, j), device_id_type=MESH)
    g_copy.wait()
    gall[0, y] = green[...].T
    pl.semaphore_wait(barrier, groups * vec_count)

    for k in range(1, groups):
        gz(k).start()

    def first_service(k):
        gz(k).wait_recv()
        gx(k).start()
        gy(k, 0).start()

    def second_service(k, odd):
        gx(k).wait_recv()
        gc0(k).start()
        if odd:
            gy(k, 0).wait_recv()
            gx_other(k).start()
        else:
            gy(k, 1).start()

    def third_service(k, odd):
        if odd:
            gx_other(k).wait_recv()
        else:
            gy(k, 0).wait_recv()
            gy(k, 1).wait_recv()
        gc1(k).start()

    first_service(1)
    if groups > 2:
        first_service(2)
    gy_first().start()
    second_service(1, True)
    if groups > 2:
        second_service(2, False)
        first_service(3)
    third_service(1, True)
    l_copy.wait()

    def columns(xq, cq):
        return pl.ds(pl.multiple_of((xq * 2 + cq) * quarter, quarter), quarter)

    def product(xq):
        cols = pl.ds(pl.multiple_of(xq * half, half), half)
        prod[...] = jnp.dot(
            inter[...],
            l_ref[:, :, cols].reshape(vectors * el, half),
            preferred_element_type=jnp.float32,
        )

    def prod_part(cq):
        return prod[:, pl.ds(pl.multiple_of(cq * quarter, quarter), quarter)]

    def serve(service, k):
        for odd in (True, False):

            @pl.when((k < groups) & (lax.rem(k, 2) == int(odd)))
            def _():
                service(k, odd)


    f32, bf = jnp.float32, jnp.bfloat16
    hq = quarter // 2

    def y_stage(k):
        rx(k, 0).wait_recv()
        a2_out[k] = (own[k, 1, rows_other, :hq] + a1_in[k, rows_other].astype(f32)).astype(bf)
        ry(k, 1).start()
        ry(k, 0).wait_recv()
        b2_out[k] = (own[k, 0, rows_me, hq:] + b1_in[k, 0].astype(f32)).astype(bf)
        rx(k, 1).start()
        kept[k, :, :hq] = own[k, 1, rows_me, :hq] + a1_in[k, rows_me].astype(f32)
        kept[k, :, hq:] = own[k, 1, rows_me, hq:] + b1_in[k, 1].astype(f32)

    def z_stage(k):
        ry(k, 1).wait_recv()
        kept[k, :, :hq] += a2_in[k].astype(f32)
        rx(k, 1).wait_recv()
        kept[k, :, hq:] += b2_in[k].astype(f32)

        @pl.when(k > 0)
        def _():
            z_out[k] = kept[k].astype(jnp.bfloat16)
            rz(k).start()

        energy = jnp.sum(kept[k] * gall[k, y, columns(x, c)].astype(jnp.float32).T)
        ebuf[k, vec] = jnp.full(ebuf.shape[2:], energy, jnp.float32)
        for j in range(1, vec_count):
            energy_send(k, j).start()

        @pl.when(k > 0)
        def _():
            energy_send(k, 0).start()

    chunk = vectors

    def step(s, carry):
        k = lax.rem(s + 1, groups)
        gc1(k).wait_recv()

        @pl.when(k > 0)
        def _():
            gc0(k).wait_recv()

        for first in range(0, vectors, chunk):
            block = lax.dot_general(
                l_ref[first : first + chunk].reshape(chunk * el, norb),
                jnp.concatenate([gall[k, 0], gall[k, 1]], axis=1),
                (((1,), (0,)), ((), ())),
                preferred_element_type=jnp.float32,
            ).astype(jnp.bfloat16)
            for g in range(chunk):
                for w in range(2):
                    inter[w * el : (w + 1) * el, (first + g) * el : (first + g + 1) * el] = block[
                        g * el : (g + 1) * el, w * el : (w + 1) * el
                    ]

        serve(third_service, s + 2)
        serve(second_service, s + 3)

        @pl.when(s > 0)
        def _():
            y_stage(s)

        product(1 - x)
        core_out[k, 0] = prod_part(1 - c).astype(bf)
        rc(k, 0).start()
        own[k, 0] = prod_part(c)
        product(x)
        core_out[k, 1] = prod_part(1 - c).astype(bf)
        rc(k, 1).start()
        rc(k, 0).wait_recv()
        own[k, 0] += core_in[k, 0].astype(f32)
        a1_out[k] = own[k, 0, :, :hq].astype(bf)
        rx(k, 0).start()
        rc(k, 1).wait_recv()
        own[k, 1] = prod_part(c) + core_in[k, 1].astype(f32)
        for n in range(2):
            b1_out[k, n] = own[k, n, rows_other, hq:].astype(bf)
        ry(k, 0).start()

        @pl.when(s + 4 < groups)
        def _():
            first_service(s + 4)

        @pl.when(s == 0)
        def _():
            gy_first().wait_recv()
            gc1(0).start()

        @pl.when(s > 0)
        def _():
            z_stage(s)

        return carry

    lax.fori_loop(0, groups, step, 0)
    y_stage(0)
    z_stage(0)

    total = kept[0]
    for k in range(1, groups):
        rz(k).wait_recv()
        total = total + z_in[k].astype(jnp.float32)
    grad_ref[...] = total * grad_scale

    e_in[0, vec] = ebuf[0, vec]
    for k in range(groups):
        for j in range(vec_count):
            if k + j > 0:
                energy_send(k, j).wait_recv()
    energies = jnp.zeros(e_in.shape[2:], jnp.float32)
    for k in range(groups):
        for n in range(vec_count):
            energies = energies + e_in[k, n]
    energy_ref[0] = jnp.max(energies) * energy_scale

    gy_first().wait_send()
    gc1(0).wait_send()
    for k in range(groups):
        for n in range(2):
            rc(k, n).wait_send()
            rx(k, n).wait_send()
            ry(k, n).wait_send()
        for j in range(vec_count):
            if k + j > 0:
                energy_send(k, j).wait_send()
        if k > 0:
            gz(k).wait_send()
            gx(k).wait_send()
            gy(k, 0).wait_send()
            (gx_other(k) if k % 2 else gy(k, 1)).wait_send()
            gc0(k).wait_send()
            gc1(k).wait_send()
            rz(k).wait_send()


def shards(cholesky_factors, walker_green):
    blk_count = lax.axis_size("blk")
    vec_count = lax.axis_size("vec")
    vectors, el, norb = cholesky_factors.shape
    vector_total = vectors * blk_count * vec_count
    groups = blk_count // 2
    assert vec_count == 4 and groups > 1 and groups & (groups - 1) == 0
    quarter = norb // vec_count
    hq = quarter // 2
    bf, f32 = jnp.bfloat16, jnp.float32
    dma = pltpu.SemaphoreType.DMA
    flops = 4 * blk_count * vectors * el * el * norb
    gradient, energy = pl.pallas_call(
        functools.partial(
            kernel, groups, vec_count, -0.5 / (el * vector_total), 1.0 / math.sqrt(vector_total)
        ),
        out_shape=(
            jax.ShapeDtypeStruct((el, quarter), f32),
            jax.ShapeDtypeStruct((1,), f32),
        ),
        in_specs=[pl.BlockSpec(memory_space=pl.ANY)] * 2,
        out_specs=(
            pl.BlockSpec(memory_space=pltpu.VMEM),
            pl.BlockSpec(memory_space=pltpu.SMEM),
        ),
        scratch_shapes=[
            pltpu.VMEM((vectors, el, norb), bf),
            pltpu.VMEM((el, norb), bf),
            pltpu.VMEM((groups, 2, norb, el), bf),
            pltpu.VMEM((2 * el, vectors * el), bf),
            pltpu.VMEM((2 * el, norb // 2), f32),
            pltpu.VMEM((groups, 2, 2 * el, quarter), bf),
            pltpu.VMEM((groups, 2, 2 * el, quarter), bf),
            pltpu.VMEM((groups, 2 * el, hq), bf),
            pltpu.VMEM((groups, 2 * el, hq), bf),
            pltpu.VMEM((groups, 2, el, hq), bf),
            pltpu.VMEM((groups, 2, el, hq), bf),
            pltpu.VMEM((groups, 2, 2 * el, quarter), f32),
            pltpu.VMEM((groups, el, hq), bf),
            pltpu.VMEM((groups, el, hq), bf),
            pltpu.VMEM((groups, el, hq), bf),
            pltpu.VMEM((groups, el, hq), bf),
            pltpu.VMEM((groups, el, quarter), f32),
            pltpu.VMEM((groups, el, quarter), bf),
            pltpu.VMEM((groups, el, quarter), bf),
            pltpu.VMEM((groups, vec_count, 8, 128), f32),
            pltpu.VMEM((groups, vec_count, 8, 128), f32),
            dma, dma,
        ]
        + [dma((groups,))] * 10
        + [dma((groups, 2))] * 8
        + [dma((groups, vec_count))] * 2,
        compiler_params=pltpu.CompilerParams(
            collective_id=0, has_side_effects=True, vmem_limit_bytes=56 * 1024 * 1024
        ),
        cost_estimate=pl.CostEstimate(
            flops=flops, bytes_accessed=2 * vectors * el * norb, transcendentals=0
        ),
        name="exchange",
    )(cholesky_factors, walker_green)
    return gradient[None], energy


def solution(mesh):
    return jax.shard_map(
        shards,
        mesh=mesh,
        in_specs=(P(("blk", "vec"), None, None), P("blk", None, None)),
        out_specs=(P("blk", None, "vec"), P("blk")),
        check_vma=False,
    )
```
